256 devices in a mesh: ctx: 32 (over y, z), fsdp: 8 (over x, core).
Axes of the slice: x: 4, y: 4, z: 8, core: 2. Of those that a mesh axis runs over, the one named last changes fastest.
Arguments:
- tokens: bfloat16 [8, 4096, 2560], P('fsdp', 'ctx'), may hold values from -10 to 10
- gate_input: bfloat16 [8, 4096, 3456], P('fsdp', 'ctx'), may hold values from -6 to 6
- segment_ids: int32 [8, 4096], P('fsdp', 'ctx'), may hold values from 0 to 7, never falling along the last dimension, each value on 1 to 1024 neighbouring positions
- in_weight: bfloat16 [2560, 3456], P('ctx', 'fsdp'), may hold values from -0.125 to 0.125
- conv_weight: float32 [4, 3456], replicated, may hold values from -3 to 3
- conv_bias: float32 [3456], replicated, may hold values from -3 to 3
- gate_a: bfloat16 [27, 128, 128], replicated, may hold values from -0.5 to 0.5
- gate_i: bfloat16 [27, 128, 128], replicated, may hold values from -0.5 to 0.5
- bias_a: float32 [3456], replicated, may hold values from -4 to -2
- bias_i: float32 [3456], replicated, may hold values from -4 to 4
- decay_rate: float32 [3456], replicated, as said below
Outputs:
- gated: bfloat16 [8, 4096, 3456], P('fsdp', 'ctx')
The draws below stay inside these ranges and needn't reach their ends.
Inputs may be any that keep to these rules, and one draw needn't show every extreme that they name: `decay_rate`: positive.
All inputs are finite; a program needn't handle non-finite values.
Results may differ from the reference program's by a relative error of at most 0.0075.
Values may be sent and summed in bfloat16 or wider, within the bound.
No kernel may reach another device: no remote copies, remote signals or barrier semaphores. Data moves between devices by JAX's collectives and lax.ppermute only.
A program may use at most 128 MiB of HBM per device.

```python
import math
import jax
import jax.numpy as jnp
import numpy as np
from jax import lax

D = 2560
R = 3456
BLOCK = 128
HEADS = 27
TAPS = 4
DOCS = 8
TOK_DEV = 128
SEQ = 4096
STREAMS = 8


def draw_decay_rate(key, part):
    key = jax.random.fold_in(key, 11)
    pick_key, slow_key, fast_key = jax.random.split(key, 3)
    share = 0.5
    chooser = jax.random.uniform(pick_key, (R,), jnp.float32)
    slow_rate = jnp.exp(jax.random.uniform(slow_key, (R,), jnp.float32, jnp.log(2.0), jnp.log(10.0))) / (8.0 * SEQ)
    fast_rate = jnp.exp(jax.random.uniform(fast_key, (R,), jnp.float32, jnp.log(0.2), jnp.log(1.0))) / 8.0
    return jnp.where(chooser < share, slow_rate, fast_rate).astype(jnp.float32)


def draw_tokens(key, part):
    key = jax.random.fold_in(key, 23)
    noise_key, pick_key, level_key = jax.random.split(key, 3)
    blocks = SEQ // TOK_DEV
    stream_keys = jax.random.split(pick_key, STREAMS)
    order = jax.vmap(lambda one_key: jax.random.permutation(one_key, blocks))(stream_keys)
    loud = order < blocks // 2
    level = jax.random.uniform(level_key, (STREAMS, blocks), jnp.float32)
    quiet_amp = jnp.exp(jnp.log(0.3) + level * jnp.log(2.0))
    loud_amp = jnp.exp(jnp.log(1.2) + level * jnp.log(2.5 / 1.2))
    amplitude = jnp.where(loud, loud_amp, quiet_amp)
    amplitude = jnp.repeat(amplitude, TOK_DEV, axis=1)[:, :, None]
    noise = jnp.clip(jax.random.normal(noise_key, (STREAMS, SEQ, D), jnp.float32), -4.0, 4.0)
    return (noise * amplitude).astype(jnp.bfloat16)


def block_levels(own_key, shape, shards, least, top_value):
    gain = 1.0
    for axis_at, blocks in shards:
        heights = jax.random.uniform(jax.random.fold_in(jax.random.fold_in(own_key, 6), axis_at), (blocks,), jnp.float32, least / len(shards), top_value / len(shards))
        gain = gain * jnp.repeat(jnp.exp(heights), shape[axis_at] // blocks).reshape((-1,) + (1,) * (len(shape) - 1 - axis_at))
    return gain


def split_up(amount, total, bound, skew):
    portions = [(1 << 20) // math.isqrt(standing ** skew) + 1 for standing in range(2, amount + 1)]
    surplus, counts = total - bound - (amount - 1), [1] * (amount - 1)
    while surplus > 0:
        movable = [i for i in range(amount - 1) if counts[i] < bound]
        whole, remaining = sum([portions[i] for i in movable]), surplus
        for i in movable:
            extra = min(bound - counts[i], max(1, remaining * portions[i] // whole), surplus)
            counts[i] = counts[i] + extra
            surplus = surplus - extra
    return np.array([bound] + counts)


def uneven_parts(rng, number_of, total, bound, slope):
    if number_of == 2:
        one = jax.random.randint(rng, (), max(1, total - bound), min(bound, total - 1) + 1)
        return jnp.stack([one, total - one])
    lengths = jnp.asarray(split_up(number_of, total, bound, slope), jnp.int32)
    couples = (number_of - 1) // 2
    giver, taker = lengths[1:1 + 2 * couples:2], lengths[2:2 + 2 * couples:2]
    margin = jnp.minimum(giver - 1, bound - taker)
    passed = jax.random.randint(jax.random.fold_in(rng, 1), (couples,), 0, 1 << 20) % (margin + 1)
    lengths = lengths.at[1:1 + 2 * couples:2].set(giver - passed).at[2:2 + 2 * couples:2].set(taker + passed)
    return lengths[jax.random.permutation(jax.random.fold_in(rng, 2), number_of)]


def centred(key, shape, spread, limit, cuts=(), held_as=jnp.bfloat16):
    drawn = spread * jax.random.normal(key, shape, jnp.float32)
    if cuts:
        drawn = drawn * block_levels(key, shape, cuts, -0.22, 0.18)
    return jnp.clip(drawn, -limit, limit).astype(held_as)


def setup_inputs(seed: int = 0) -> dict:
    seeds = jax.random.split(jax.random.key(seed), 12)
    tokens = draw_tokens(jax.random.fold_in(seeds[11], 71), 0)
    gate_input = centred(seeds[1], (STREAMS, SEQ, R), 1.0, 6.0, ((0, 8), (1, 32)))
    segment_ids = jax.vmap(lambda own: jnp.searchsorted(jnp.cumsum(uneven_parts(own, DOCS, SEQ, SEQ // 4, 1)), jnp.arange(SEQ), side="right"))(jax.random.split(seeds[2], STREAMS)).reshape((STREAMS, SEQ)).astype(jnp.int32)
    in_weight = centred(seeds[3], (D, R), D ** -0.5, 0.125, ((0, 32), (1, 8)))
    conv_weight = centred(seeds[4], (TAPS, R), 0.5, 3.0, (), jnp.float32)
    conv_bias = centred(seeds[5], (R,), 0.5, 3.0, (), jnp.float32)
    gate_a = centred(seeds[6], (HEADS, BLOCK, BLOCK), BLOCK ** -0.5, 0.5)
    gate_i = centred(seeds[7], (HEADS, BLOCK, BLOCK), BLOCK ** -0.5, 0.5)
    bias_a = jnp.clip(jax.random.uniform(seeds[8], (R,), jnp.float32, -4.0, -2.0), -4.0, -2.0)
    bias_i = centred(seeds[9], (R,), 1.0, 4.0, (), jnp.float32)
    decay_rate = draw_decay_rate(jax.random.fold_in(seeds[11], 71), 0)
    return dict(tokens=tokens, gate_input=gate_input, segment_ids=segment_ids, in_weight=in_weight, conv_weight=conv_weight, conv_bias=conv_bias, gate_a=gate_a, gate_i=gate_i, bias_a=bias_a, bias_i=bias_i, decay_rate=decay_rate)


def combine_pairs(earlier, later):
    return (earlier[0] * later[0], later[0] * earlier[1] + later[1])

def one_stream(tokens_row, gate_row, seg_row, in_weight, conv_weight, conv_bias, gate_a, gate_i, bias_a, bias_i, decay_rate):
    length = seg_row.shape[0]
    projected = jnp.dot(tokens_row, in_weight, preferred_element_type=jnp.float32).astype(jnp.bfloat16)
    proj_wide = projected.astype(jnp.float32)
    conv = conv_weight[0][None, :] * proj_wide + conv_bias[None, :]
    for back in range(1, TAPS):
        shifted = jnp.concatenate([jnp.zeros((back, R), jnp.float32), proj_wide[:-back]], axis=0)
        shifted_ids = jnp.concatenate([jnp.full((back,), -1, jnp.int32), seg_row[:-back]], axis=0)
        valid = (shifted_ids == seg_row)[:, None]
        conv = conv + conv_weight[back][None, :] * jnp.where(valid, shifted, jnp.float32(0.0))
    conv = conv.astype(jnp.bfloat16)
    conv_wide = conv.astype(jnp.float32)
    blocked = conv_wide.reshape(length, HEADS, BLOCK)
    rgate = jax.nn.sigmoid(jnp.einsum('thi,hij->thj', blocked, gate_a.astype(jnp.float32)).reshape(length, R) + bias_a[None, :])
    igate = jax.nn.sigmoid(jnp.einsum('thi,hij->thj', blocked, gate_i.astype(jnp.float32)).reshape(length, R) + bias_i[None, :])
    logdecay = -8.0 * decay_rate[None, :] * rgate
    decay = jnp.exp(logdecay)
    previous_ids = jnp.concatenate([jnp.full((1,), -1, jnp.int32), seg_row[:-1]], axis=0)
    reset = (seg_row != previous_ids)[:, None]
    factor = jnp.where(reset, jnp.float32(1.0), jnp.sqrt(-jnp.expm1(2.0 * logdecay)))
    inflow = factor * igate * conv_wide
    keep = jnp.where(reset, jnp.float32(0.0), decay)
    products, state = lax.associative_scan(combine_pairs, (keep, inflow), axis=0)
    gelu_gate = jax.nn.gelu(gate_row.astype(jnp.float32), approximate=True)
    return (state * gelu_gate).astype(jnp.bfloat16)

def reference(tokens, gate_input, segment_ids, in_weight, conv_weight, conv_bias, gate_a, gate_i, bias_a, bias_i, decay_rate):

    def per_stream(items):
        return one_stream(items[0], items[1], items[2], in_weight, conv_weight, conv_bias, gate_a, gate_i, bias_a, bias_i, decay_rate)
    return lax.map(per_stream, (tokens, gate_input, segment_ids))
```

```python
import functools

import jax
import jax.numpy as jnp
from jax import lax
from jax.experimental import pallas as pl
from jax.experimental.pallas import tpu as pltpu
from jax.sharding import Mesh
from jax.sharding import PartitionSpec as P

F32 = jnp.float32
BF16 = jnp.bfloat16
VMEM = pl.BlockSpec(memory_space=pltpu.VMEM)
SMEM = pl.BlockSpec(memory_space=pltpu.SMEM)

LENGTH = 128
WIDTH = 3456
DEPTH = 2560
COLS = 432
HEAD = 128
HEADS = 27
SPAN = 16
HALO = 8
PACK = COLS + 32
CUT = 256


def shift(value, axis, by):
    count = lax.axis_size(axis)
    return lax.ppermute(value, axis, [(i, (i + by) % count) for i in range(count)])


def flip(value):
    return lax.ppermute(value, "c", [(0, 1), (1, 0)])


def ring(value, axis, cut):
    back = shift(value, axis, 1)
    ahead = shift(value, axis, -1)
    first = shift(back[:cut], axis, 1)
    second = shift(ahead[cut:], axis, -1)
    return value, back, ahead, first, second


def prepare_kernel(gate_ref, ids_ref, gelu_ref, mask_ref, ids_scr):
    def head(h, carry):
        lanes = pl.ds(pl.multiple_of(h * HEAD, HEAD), HEAD)
        gelu_ref[h] = jax.nn.gelu(gate_ref[:, lanes].astype(F32), approximate=True)
        return carry

    lax.fori_loop(0, HEADS, head, 0)
    prior = jnp.broadcast_to(ids_ref[0:1, :], (LENGTH, LENGTH)).T
    own = jnp.broadcast_to(ids_ref[1:2, :], (LENGTH, LENGTH)).T
    ids_scr[0:HALO, :] = prior[LENGTH - HALO :, :]
    ids_scr[HALO:, :] = own
    for k in range(SPAN):
        here = ids_scr[pl.ds(HALO + k, 8, stride=SPAN), :]
        for back in range(1, 4):
            there = ids_scr[pl.ds(HALO + k - back, 8, stride=SPAN), :]
            same = (here == there).astype(F32)
            mask_ref[back, 8 * k : 8 * k + 8, :] = same
            if back == 1:
                mask_ref[0, 8 * k : 8 * k + 8, :] = same


def project_kernel(at_ref, t0, t1, t2, t3, w0, w1, w2, w3, w4, out_ref, acc_ref, wide_ref):
    x, c, y = at_ref[0], at_ref[1], at_ref[2]
    steps = (
        (lax.rem(y, 4) * 640, 640, w0),
        (lax.rem(y + 3, 4) * 640, 640, w1),
        (lax.rem(y + 1, 4) * 640, 640, w2),
        (lax.rem(y + 2, 4) * 640, CUT, w3),
        (lax.rem(y + 2, 4) * 640 + CUT, 640 - CUT, w4),
    )
    for back, t_ref in ((0, t0), (1, t1), (3, t2), (2, t3)):
        total = None
        for start, size, w_ref in steps:
            part = jnp.dot(
                t_ref[:, pl.ds(pl.multiple_of(start, 128), size)],
                w_ref[...],
                preferred_element_type=F32,
            )
            total = part if total is None else total + part
        acc_ref[...] = total
        for other in range(2):
            stream = lax.rem(x + 4 - back, 4) * 2 + (c if other == 0 else 1 - c)
            top = other * (LENGTH + HALO)
            wide_ref[:, 0:COLS] = acc_ref[top : top + LENGTH + HALO, :]
            for j in range(4):
                block = wide_ref[0:LENGTH, j * 128 : (j + 1) * 128].T.astype(BF16)
                size = min(128, COLS - j * 128)
                out_ref[stream, j * 128 : j * 128 + size, :] = block[:size]
            for j in range(2):
                pair = [
                    wide_ref[LENGTH : LENGTH + HALO, (2 * j + i) * 128 : (2 * j + i + 1) * 128]
                    for i in range(2)
                ]
                out_ref[stream, COLS + 16 * j : COLS + 16 * j + 16, :] = jnp.concatenate(
                    pair, axis=0
                ).astype(BF16)


def recur_kernel(
    got_ref, mask_ref, gelu_ref, par_ref, gates_ref, state_ref, prod_ref, end_ref, x_scr
):
    ahead = []
    for f in range(8):
        packed = got_ref[f, COLS:PACK, :].astype(F32)
        ahead += [packed[8 * j : 8 * j + 8, : min(128, COLS - 128 * j)] for j in range(4)]
    ahead = jnp.concatenate(ahead, axis=1)
    for h in range(HEADS):
        f, low = (h * HEAD) // COLS, (h * HEAD) % COLS
        size = min(HEAD, COLS - low)
        block = got_ref[f, low : low + size, :].astype(F32)
        if size < HEAD:
            rest = got_ref[f + 1, 0 : HEAD - size, :].astype(F32)
            block = jnp.concatenate([block, rest], axis=0)
        x_scr[h, 0:HALO, :] = ahead[:, h * HEAD : (h + 1) * HEAD]
        x_scr[h, HALO:, :] = block.T

    row = lax.broadcasted_iota(jnp.int32, (8, HEAD), 0)

    def head(h, carry):
        lanes = pl.ds(pl.multiple_of(h * HEAD, HEAD), HEAD)
        par = [par_ref[i : i + 1, lanes] for i in range(8)]
        shifted = {
            off: x_scr[h, pl.ds(HALO + off, 8, stride=SPAN), :] for off in range(-3, SPAN)
        }
        conv = []
        for k in range(SPAN):
            total = par[0] * shifted[k] + par[4]
            for back in range(1, 4):
                valid = mask_ref[back, 8 * k : 8 * k + 8, :]
                total = total + par[back] * (shifted[k - back] * valid)
            conv.append(total)
        conv = jnp.concatenate(conv, axis=0).astype(BF16)
        both = jnp.dot(conv, gates_ref[h], preferred_element_type=F32)
        rgate = jax.nn.sigmoid(both[:, :HEAD] + par[5])
        igate = jax.nn.sigmoid(both[:, HEAD:] + par[6])
        logdecay = par[7] * rgate
        decay = jnp.exp(logdecay)
        same = mask_ref[0]
        twice = 2.0 * logdecay
        series = 1.0 + twice * (
            1 / 2
            + twice
            * (1 / 6 + twice * (1 / 24 + twice * (1 / 120 + twice * (1 / 720 + twice * (1 / 5040)))))
        )
        lost = jnp.where(twice > -0.5, -twice * series, 1.0 - decay * decay)
        factor = jnp.where(same > 0.5, jnp.sqrt(lost), 1.0)
        inflow = factor * igate * conv.astype(F32)
        keep = decay * same
        prods, states = [keep[0:8]], [inflow[0:8]]
        for k in range(1, SPAN):
            part = keep[8 * k : 8 * k + 8]
            prods.append(part * prods[-1])
            states.append(part * states[-1] + inflow[8 * k : 8 * k + 8])
        prod, state = prods[-1], states[-1]
        for by in (1, 2, 4):
            before_prod = jnp.where(row >= by, pltpu.roll(prod, by, 0), 1.0)
            before_state = jnp.where(row >= by, pltpu.roll(state, by, 0), 0.0)
            state = prod * before_state + state
            prod = prod * before_prod
        end_ref[0:1, lanes] = prod[7:8]
        end_ref[1:2, lanes] = state[7:8]
        in_prod = jnp.where(row >= 1, pltpu.roll(prod, 1, 0), 1.0)
        in_state = jnp.where(row >= 1, pltpu.roll(state, 1, 0), 0.0)
        for k in range(SPAN):
            at = pl.ds(k, 8, stride=SPAN)
            gelu = gelu_ref[h, at, :]
            state_ref[h, at, :] = (states[k] + prods[k] * in_state) * gelu
            prod_ref[h, at, :] = (prods[k] * in_prod) * gelu
        return carry

    lax.fori_loop(0, HEADS, head, 0)


def finish_kernel(state_ref, prod_ref, in_ref, out_ref):
    def head(h, carry):
        lanes = pl.ds(pl.multiple_of(h * HEAD, HEAD), HEAD)
        out_ref[:, lanes] = (state_ref[h] + prod_ref[h] * in_ref[:, lanes]).astype(BF16)
        return carry

    lax.fori_loop(0, HEADS, head, 0)


def call(kernel, outs, ins, scratch=(), flops=0, moved=0):
    return pl.pallas_call(
        kernel,
        out_shape=outs,
        in_specs=ins,
        out_specs=jax.tree.map(lambda _: VMEM, outs),
        scratch_shapes=list(scratch),
        compiler_params=pltpu.CompilerParams(vmem_limit_bytes=48 * 2**20),
        cost_estimate=pl.CostEstimate(flops=flops, bytes_accessed=moved, transcendentals=0),
    )


def joined(earlier, later):
    return jnp.concatenate(
        [earlier[:1] * later[:1], later[:1] * earlier[1:] + later[1:]], axis=0
    )


def body(
    tokens,
    gate_input,
    segment_ids,
    in_weight,
    conv_weight,
    conv_bias,
    gate_a,
    gate_i,
    bias_a,
    bias_i,
    decay_rate,
):
    ctx = ("y", "z")
    own = tokens[0]
    at = jnp.stack([lax.axis_index("x"), lax.axis_index("c"), lax.axis_index("y")]).astype(
        jnp.int32
    )

    column = lax.all_to_all(
        jnp.broadcast_to(in_weight[None], (8,) + in_weight.shape), "z", 0, 0, tiled=True
    ).reshape(-1, in_weight.shape[1])
    weights = ring(column, "y", CUT)

    rows = jnp.concatenate([own, shift(own[-HALO:], ctx, 1)], axis=0)
    here, back, ahead, first, second = ring(rows, "x", 64)
    far = jnp.concatenate([first, second], axis=0)
    streams = [jnp.concatenate([t, flip(t)], axis=0) for t in (here, back, ahead, far)]

    ids = segment_ids.astype(BF16)
    prior = shift(ids, ctx, 1).astype(F32)
    prior = jnp.where(lax.axis_index(ctx) == 0, F32(-1.0), prior)
    ids = jnp.concatenate([prior, segment_ids.astype(F32)], axis=0)
    gelu, masks = call(
        prepare_kernel,
        (
            jax.ShapeDtypeStruct((HEADS, LENGTH, HEAD), F32),
            jax.ShapeDtypeStruct((4, LENGTH, HEAD), F32),
        ),
        [VMEM] * 2,
        [pltpu.VMEM((LENGTH + HALO, HEAD), F32)],
        moved=2_700_000,
    )(gate_input[0], ids)
    params = jnp.concatenate(
        [
            conv_weight,
            conv_bias[None],
            bias_a[None],
            bias_i[None],
            -8.0 * decay_rate[None],
        ],
        axis=0,
    )
    gates = jnp.concatenate([gate_a, gate_i], axis=2)

    sent = call(
        project_kernel,
        jax.ShapeDtypeStruct((8, PACK, 128), BF16),
        [SMEM] + [VMEM] * 9,
        [
            pltpu.VMEM((2 * (LENGTH + HALO), COLS), F32),
            pltpu.VMEM((LENGTH + HALO, 512), F32),
        ],
        flops=2 * 1088 * 2560 * 432,
        moved=8_000_000,
    )(at, *streams, *weights)
    got = lax.all_to_all(sent, ("x", "c"), 0, 0, tiled=True)
    states, prods, ends = call(
        recur_kernel,
        (
            jax.ShapeDtypeStruct((HEADS, LENGTH, HEAD), F32),
            jax.ShapeDtypeStruct((HEADS, LENGTH, HEAD), F32),
            jax.ShapeDtypeStruct((2, WIDTH), F32),
        ),
        [VMEM] * 5,
        [pltpu.VMEM((HEADS, LENGTH + HALO, HEAD), F32)],
        flops=2 * 128 * 3456 * 256,
        moved=8_000_000,
    )(got, masks, gelu, params, gates)

    two = joined(shift(ends, ctx, 1), ends)
    pairs = [shift(two, ctx, by) for by in (7, 5, 3, 1)]
    incoming = functools.reduce(joined, pairs)[1:]
    out = call(
        finish_kernel,
        jax.ShapeDtypeStruct((LENGTH, WIDTH), BF16),
        [VMEM] * 3,
        moved=4_400_000,
    )(states, prods, incoming)
    return out[None]


def solution(mesh):
    fine = Mesh(mesh.devices.reshape(4, 8, 4, 2), ("y", "z", "x", "c"))
    ctx, fsdp = ("y", "z"), ("x", "c")
    placed = (
        P(fsdp, ctx, None),
        P(fsdp, ctx, None),
        P(fsdp, ctx),
        P(ctx, fsdp),
        P(),
        P(),
        P(),
        P(),
        P(),
        P(),
        P(),
    )
    return jax.shard_map(
        body, mesh=fine, in_specs=placed, out_specs=P(fsdp, ctx, None), check_vma=False
    )
```

```python
import functools

import jax
import jax.numpy as jnp
from jax import lax
from jax.experimental import pallas as pl
from jax.experimental.pallas import tpu as pltpu
from jax.sharding import Mesh
from jax.sharding import PartitionSpec as P

F32 = jnp.float32
BF16 = jnp.bfloat16
VMEM = pl.BlockSpec(memory_space=pltpu.VMEM)
SMEM = pl.BlockSpec(memory_space=pltpu.SMEM)

LENGTH = 128
WIDTH = 3456
DEPTH = 2560
COLS = 432
HEAD = 128
HEADS = 27
SPAN = 16
HALO = 8
PACK = COLS + 32
FULL = 512
CUT = 256
ROWS = LENGTH + HALO


def shift(value, axis, by):
    count = lax.axis_size(axis)
    return lax.ppermute(value, axis, [(i, (i + by) % count) for i in range(count)])


def flip(value):
    return lax.ppermute(value, "c", [(0, 1), (1, 0)])


def prepare_kernel(gate_ref, ids_ref, gelu_ref, mask_ref, ids_scr):
    def head(h, carry):
        lanes = pl.ds(pl.multiple_of(h * HEAD, HEAD), HEAD)
        gelu_ref[h] = jax.nn.gelu(gate_ref[:, lanes].astype(F32), approximate=True)
        return carry

    lax.fori_loop(0, HEADS, head, 0)
    prior = jnp.broadcast_to(ids_ref[0:1, :], (LENGTH, LENGTH)).T
    own = jnp.broadcast_to(ids_ref[1:2, :], (LENGTH, LENGTH)).T
    ids_scr[0:HALO, :] = prior[LENGTH - HALO :, :]
    ids_scr[HALO:, :] = own
    for k in range(SPAN):
        here = ids_scr[pl.ds(HALO + k, 8, stride=SPAN), :]
        for back in range(1, 4):
            there = ids_scr[pl.ds(HALO + k - back, 8, stride=SPAN), :]
            same = (here == there).astype(F32)
            mask_ref[back, 8 * k : 8 * k + 8, :] = same
            if back == 1:
                mask_ref[0, 8 * k : 8 * k + 8, :] = same


def copies(pairs, sems):
    made = [
        pltpu.make_async_copy(src, dst, sems.at[i]) for i, (src, dst) in enumerate(pairs)
    ]
    for copy in made:
        copy.start()
    return made


def project_kernel(at_ref, t0, t1, t2, t3, *refs):
    weights, part_ref = refs[:6], refs[6]
    y = at_ref[2]
    for i, t_ref in enumerate((t0, t1, t2, t3)):
        for half in range(2):
            total = None
            for j, back in enumerate((0, 3, 1)):
                start = pl.multiple_of(lax.rem(y + back, 4) * 640, 128)
                part = jnp.dot(
                    t_ref[:, pl.ds(start, 640)],
                    weights[2 * j + half][...],
                    preferred_element_type=F32,
                )
                total = part if total is None else total + part
            part_ref[i, half] = total


def pack_kernel(at_ref, part_ref, t0, t1, t2, t3, *refs):
    weights, outs = refs[:4], refs[4:8]
    wide_ref = refs[8]
    c, y = at_ref[1], at_ref[2]
    far = lax.rem(y + 2, 4) * 640
    for i, t_ref in enumerate((t0, t1, t2, t3)):
        for half in range(2):
            total = part_ref[i, half]
            for j, (start, size) in enumerate(((far, CUT), (far + CUT, 640 - CUT))):
                total = total + jnp.dot(
                    t_ref[:, pl.ds(pl.multiple_of(start, 128), size)],
                    weights[2 * j + half][...],
                    preferred_element_type=F32,
                )
            wide_ref[...] = total
            place = c if half == 0 else 1 - c
            out_ref = outs[i]
            for j in range(4):
                block = wide_ref[0:LENGTH, j * 128 : (j + 1) * 128].T.astype(BF16)
                size = min(128, COLS - j * 128)
                out_ref[place, j * 128 : j * 128 + size, :] = block[:size]
            for j in range(2):
                pair = [
                    wide_ref[LENGTH:ROWS, (2 * j + n) * 128 : (2 * j + n + 1) * 128]
                    for n in range(2)
                ]
                out_ref[place, COLS + 16 * j : COLS + 16 * j + 16, :] = jnp.concatenate(
                    pair, axis=0
                ).astype(BF16)


def recur_kernel(
    at_ref,
    g0,
    g1,
    g2,
    g3,
    mask_ref,
    gelu_ref,
    par_ref,
    gates_ref,
    state_ref,
    prod_ref,
    end_ref,
    x_scr,
    got_ref,
    sems,
):
    x = at_ref[0]
    pairs = [
        (ref, got_ref.at[pl.ds(lax.rem(x + 4 - back, 4) * 2, 2)])
        for back, ref in ((0, g0), (1, g1), (3, g2), (2, g3))
    ]
    for copy in copies(pairs, sems):
        copy.wait()
    ahead = []
    for f in range(8):
        packed = got_ref[f, COLS:PACK, :].astype(F32)
        ahead += [packed[8 * j : 8 * j + 8, : min(128, COLS - 128 * j)] for j in range(4)]
    ahead = jnp.concatenate(ahead, axis=1)
    for h in range(HEADS):
        f, low = (h * HEAD) // COLS, (h * HEAD) % COLS
        size = min(HEAD, COLS - low)
        block = got_ref[f, low : low + size, :].astype(F32)
        if size < HEAD:
            rest = got_ref[f + 1, 0 : HEAD - size, :].astype(F32)
            block = jnp.concatenate([block, rest], axis=0)
        x_scr[h, 0:HALO, :] = ahead[:, h * HEAD : (h + 1) * HEAD]
        x_scr[h, HALO:, :] = block.T

    row = lax.broadcasted_iota(jnp.int32, (8, HEAD), 0)

    def head(h, carry):
        lanes = pl.ds(pl.multiple_of(h * HEAD, HEAD), HEAD)
        par = [par_ref[i : i + 1, lanes] for i in range(8)]
        shifted = {
            off: x_scr[h, pl.ds(HALO + off, 8, stride=SPAN), :] for off in range(-3, SPAN)
        }
        conv = []
        for k in range(SPAN):
            total = par[0] * shifted[k] + par[4]
            for back in range(1, 4):
                valid = mask_ref[back, 8 * k : 8 * k + 8, :]
                total = total + par[back] * (shifted[k - back] * valid)
            conv.append(total)
        conv = jnp.concatenate(conv, axis=0).astype(BF16)
        both = jnp.dot(conv, gates_ref[h], preferred_element_type=F32)
        rgate = jax.nn.sigmoid(both[:, :HEAD] + par[5])
        igate = jax.nn.sigmoid(both[:, HEAD:] + par[6])
        logdecay = par[7] * rgate
        decay = jnp.exp(logdecay)
        same = mask_ref[0]
        twice = 2.0 * logdecay
        series = 1.0 + twice * (
            1 / 2
            + twice
            * (1 / 6 + twice * (1 / 24 + twice * (1 / 120 + twice * (1 / 720 + twice * (1 / 5040)))))
        )
        lost = jnp.where(twice > -0.5, -twice * series, 1.0 - decay * decay)
        factor = jnp.where(same > 0.5, jnp.sqrt(lost), 1.0)
        inflow = factor * igate * conv.astype(F32)
        keep = decay * same
        prods, states = [keep[0:8]], [inflow[0:8]]
        for k in range(1, SPAN):
            part = keep[8 * k : 8 * k + 8]
            prods.append(part * prods[-1])
            states.append(part * states[-1] + inflow[8 * k : 8 * k + 8])
        prod, state = prods[-1], states[-1]
        for by in (1, 2, 4):
            before_prod = jnp.where(row >= by, pltpu.roll(prod, by, 0), 1.0)
            before_state = jnp.where(row >= by, pltpu.roll(state, by, 0), 0.0)
            state = prod * before_state + state
            prod = prod * before_prod
        end_ref[0:1, lanes] = prod[7:8]
        end_ref[1:2, lanes] = state[7:8]
        in_prod = jnp.where(row >= 1, pltpu.roll(prod, 1, 0), 1.0)
        in_state = jnp.where(row >= 1, pltpu.roll(state, 1, 0), 0.0)
        for k in range(SPAN):
            at = pl.ds(k, 8, stride=SPAN)
            gelu = gelu_ref[h, at, :]
            state_ref[h, at, :] = (states[k] + prods[k] * in_state) * gelu
            prod_ref[h, at, :] = (prods[k] * in_prod) * gelu
        return carry

    lax.fori_loop(0, HEADS, head, 0)


def finish_kernel(state_ref, prod_ref, in_ref, out_ref):
    def head(h, carry):
        lanes = pl.ds(pl.multiple_of(h * HEAD, HEAD), HEAD)
        out_ref[:, lanes] = (state_ref[h] + prod_ref[h] * in_ref[:, lanes]).astype(BF16)
        return carry

    lax.fori_loop(0, HEADS, head, 0)


def call(kernel, outs, ins, scratch=(), room=16, flops=0, moved=0):
    return pl.pallas_call(
        kernel,
        out_shape=outs,
        in_specs=ins,
        out_specs=jax.tree.map(lambda _: VMEM, outs),
        scratch_shapes=list(scratch),
        compiler_params=pltpu.CompilerParams(vmem_limit_bytes=room * 2**20),
        cost_estimate=pl.CostEstimate(flops=flops, bytes_accessed=moved, transcendentals=0),
    )


def joined(earlier, later):
    return jnp.concatenate(
        [earlier[:1] * later[:1], later[:1] * earlier[1:] + later[1:]], axis=0
    )


def body(
    tokens,
    gate_input,
    segment_ids,
    in_weight,
    conv_weight,
    conv_bias,
    gate_a,
    gate_i,
    bias_a,
    bias_i,
    decay_rate,
):
    ctx = ("y", "z")
    own = tokens[0]
    at = jnp.stack([lax.axis_index("x"), lax.axis_index("c"), lax.axis_index("y")]).astype(
        jnp.int32
    )

    filled = jnp.pad(in_weight, ((0, 0), (0, FULL - COLS)))
    column = lax.all_to_all(
        jnp.broadcast_to(filled[None], (8,) + filled.shape), "z", 0, 0, tiled=True
    ).reshape(-1, FULL)
    from_back = shift(column, "y", 1)
    from_ahead = shift(column, "y", -1)
    near = [column, flip(column), from_back, flip(from_back), from_ahead, flip(from_ahead)]
    first = shift(from_back[:CUT], "y", 1)
    second = shift(from_ahead[CUT:], "y", -1)
    far = [first, flip(first), second, flip(second)]

    rows = jnp.concatenate([own, shift(own[-HALO:], ctx, 1)], axis=0)
    streams = [rows, shift(rows, "x", 1), shift(rows, "x", -1), shift(rows, "x", 2)]

    ids = segment_ids.astype(BF16)
    prior = shift(ids, ctx, 1).astype(F32)
    prior = jnp.where(lax.axis_index(ctx) == 0, F32(-1.0), prior)
    ids = jnp.concatenate([prior, segment_ids.astype(F32)], axis=0)
    gelu, masks = call(
        prepare_kernel,
        (
            jax.ShapeDtypeStruct((HEADS, LENGTH, HEAD), F32),
            jax.ShapeDtypeStruct((4, LENGTH, HEAD), F32),
        ),
        [VMEM] * 2,
        [pltpu.VMEM((LENGTH + HALO, HEAD), F32)],
        moved=2_700_000,
    )(gate_input[0], ids)
    params = jnp.concatenate(
        [
            conv_weight,
            conv_bias[None],
            bias_a[None],
            bias_i[None],
            -8.0 * decay_rate[None],
        ],
        axis=0,
    )
    gates = jnp.concatenate([gate_a, gate_i], axis=2)

    part = call(
        project_kernel,
        jax.ShapeDtypeStruct((4, 2, ROWS, FULL), F32),
        [SMEM] + [VMEM] * 10,
        flops=2 * 544 * 1920 * 1024,
        moved=9_000_000,
    )(at, *streams, *near)
    sent = call(
        pack_kernel,
        [jax.ShapeDtypeStruct((2, PACK, 128), BF16)] * 4,
        [SMEM] + [VMEM] * 9,
        [pltpu.VMEM((ROWS, FULL), F32)],
        flops=2 * 544 * 640 * 1024,
        moved=7_000_000,
    )(at, part, *streams, *far)
    got = [
        sent[0],
        shift(sent[2], "x", 1),
        shift(sent[1], "x", -1),
        shift(sent[3], "x", 2),
    ]
    states, prods, ends = call(
        recur_kernel,
        (
            jax.ShapeDtypeStruct((HEADS, LENGTH, HEAD), F32),
            jax.ShapeDtypeStruct((HEADS, LENGTH, HEAD), F32),
            jax.ShapeDtypeStruct((2, WIDTH), F32),
        ),
        [SMEM] + [pl.BlockSpec(memory_space=pl.ANY)] * 4 + [VMEM] * 4,
        [
            pltpu.VMEM((HEADS, LENGTH + HALO, HEAD), F32),
            pltpu.VMEM((8, PACK, 128), BF16),
            pltpu.SemaphoreType.DMA((4,)),
        ],
        flops=2 * 128 * 3456 * 256,
        moved=8_000_000,
    )(at, *got, masks, gelu, params, gates)

    two = joined(shift(ends, ctx, 1), ends)
    pairs = [shift(two, ctx, by) for by in (7, 5, 3, 1)]
    incoming = functools.reduce(joined, pairs)[1:]
    out = call(
        finish_kernel,
        jax.ShapeDtypeStruct((LENGTH, WIDTH), BF16),
        [VMEM] * 3,
        moved=4_400_000,
    )(states, prods, incoming)
    return out[None]


def solution(mesh):
    fine = Mesh(mesh.devices.reshape(4, 8, 4, 2), ("y", "z", "x", "c"))
    ctx, fsdp = ("y", "z"), ("x", "c")
    placed = (
        P(fsdp, ctx, None),
        P(fsdp, ctx, None),
        P(fsdp, ctx),
        P(ctx, fsdp),
        P(),
        P(),
        P(),
        P(),
        P(),
        P(),
        P(),
    )
    return jax.shard_map(
        body, mesh=fine, in_specs=placed, out_specs=P(fsdp, ctx, None), check_vma=False
    )
```

```python
import functools

import jax
import jax.numpy as jnp
from jax import lax
from jax.experimental import pallas as pl
from jax.experimental.pallas import tpu as pltpu
from jax.sharding import Mesh
from jax.sharding import PartitionSpec as P

F32 = jnp.float32
BF16 = jnp.bfloat16
VMEM = pl.BlockSpec(memory_space=pltpu.VMEM)
ANY = pl.BlockSpec(memory_space=pl.ANY)
SMEM = pl.BlockSpec(memory_space=pltpu.SMEM)

LENGTH = 128
WIDTH = 3456
DEPTH = 2560
COLS = 432
HEAD = 128
HEADS = 27
SPAN = 16
HALO = 8
PACK = COLS + 32
CUT = 208
AHEAD = 4 * HALO + 16
ROWS = 4 * LENGTH + AHEAD


def shift(value, axis, by):
    count = lax.axis_size(axis)
    return lax.ppermute(value, axis, [(i, (i + by) % count) for i in range(count)])


def flip(value):
    return lax.ppermute(value, "c", [(0, 1), (1, 0)])


def prepare_kernel(at_ref, gate_ref, ids_ref, ahead_ref, gelu_ref, mask_ref, ids_scr):
    def head(h, carry):
        lanes = pl.ds(pl.multiple_of(h * HEAD, HEAD), HEAD)
        gelu_ref[h] = jax.nn.gelu(gate_ref[:, lanes].astype(F32), approximate=True)
        return carry

    lax.fori_loop(0, HEADS, head, 0)
    prior = ahead_ref[4 * HALO : AHEAD, 0:LENGTH].astype(F32)[0:1]
    prior = jnp.where(at_ref[3] == 0, -1.0, prior)
    prior = jnp.broadcast_to(prior, (LENGTH, LENGTH)).T
    own = jnp.broadcast_to(ids_ref[...].astype(F32), (LENGTH, LENGTH)).T
    ids_scr[0:HALO, :] = prior[LENGTH - HALO :, :]
    ids_scr[HALO:, :] = own
    for k in range(SPAN):
        here = ids_scr[pl.ds(HALO + k, 8, stride=SPAN), :]
        for back in range(1, 4):
            there = ids_scr[pl.ds(HALO + k - back, 8, stride=SPAN), :]
            same = (here == there).astype(F32)
            mask_ref[back, 8 * k : 8 * k + 8, :] = same
            if back == 1:
                mask_ref[0, 8 * k : 8 * k + 8, :] = same


def copies(pairs, sems):
    made = [
        pltpu.make_async_copy(src, dst, sems.at[i]) for i, (src, dst) in enumerate(pairs)
    ]
    for copy in made:
        copy.start()
    return made


def across(weight, rows):
    return lax.dot_general(
        weight, rows, (((1,), (1,)), ((), ())), preferred_element_type=F32
    )


def project_kernel(at_ref, t0, t1, t2, t3, ahead, *refs):
    weights, (part_ref, far_ref, rows_ref, sems) = refs[:6], refs[6:]
    y = at_ref[2]
    pairs = [
        (ref, rows_ref.at[pl.ds(i * LENGTH, LENGTH)]) for i, ref in enumerate((t0, t1, t2, t3))
    ] + [(ahead, rows_ref.at[pl.ds(4 * LENGTH, AHEAD)])]
    for copy in copies(pairs, sems):
        copy.wait()
    for half in range(2):
        total = None
        for j, back in enumerate((0, 3, 1)):
            start = pl.multiple_of(lax.rem(y + back, 4) * 640, 128)
            part = across(weights[2 * j + half][...], rows_ref[:, pl.ds(start, 640)])
            total = part if total is None else total + part
        part_ref[half] = total
    far_ref[...] = rows_ref[:, pl.ds(pl.multiple_of(lax.rem(y + 2, 4) * 640, 128), 640)]


def pack_kernel(at_ref, part_ref, far_ref, *refs):
    weights, outs, (all_ref, wide_ref) = refs[:4], refs[4:8], refs[8:]
    c = at_ref[1]
    for half in range(2):
        all_ref[0:CUT, :] = weights[half][...]
        all_ref[CUT:COLS, :] = weights[2 + half][...]
        total = part_ref[half] + across(all_ref[...], far_ref[...])
        place = c if half == 0 else 1 - c
        wide_ref[0:COLS, 0:AHEAD] = total[:, 4 * LENGTH :]
        turned = [wide_ref[j * 128 : (j + 1) * 128, :].T for j in range(4)]
        for i, out_ref in enumerate(outs):
            out_ref[place, 0:COLS, :] = total[:, i * LENGTH : (i + 1) * LENGTH].astype(BF16)
            for j in range(2):
                pair = [turned[2 * j + n][HALO * i : HALO * i + HALO, :] for n in range(2)]
                out_ref[place, COLS + 16 * j : COLS + 16 * j + 16, :] = jnp.concatenate(
                    pair, axis=0
                ).astype(BF16)


def recur_kernel(
    at_ref,
    g0,
    g1,
    g2,
    g3,
    mask_ref,
    gelu_ref,
    taps_ref,
    bias_ref,
    bias_a_ref,
    bias_i_ref,
    rate_ref,
    gate_a_ref,
    gate_i_ref,
    state_ref,
    prod_ref,
    end_ref,
    x_scr,
    got_ref,
    sems,
):
    x = at_ref[0]
    pairs = [
        (ref, got_ref.at[pl.ds(lax.rem(x + 4 - back, 4) * 2, 2)])
        for back, ref in ((0, g0), (1, g1), (3, g2), (2, g3))
    ]
    for copy in copies(pairs, sems):
        copy.wait()
    ahead = []
    for f in range(8):
        packed = got_ref[f, COLS:PACK, :].astype(F32)
        ahead += [packed[8 * j : 8 * j + 8, : min(128, COLS - 128 * j)] for j in range(4)]
    ahead = jnp.concatenate(ahead, axis=1)
    for h in range(HEADS):
        f, low = (h * HEAD) // COLS, (h * HEAD) % COLS
        size = min(HEAD, COLS - low)
        block = got_ref[f, low : low + size, :].astype(F32)
        if size < HEAD:
            rest = got_ref[f + 1, 0 : HEAD - size, :].astype(F32)
            block = jnp.concatenate([block, rest], axis=0)
        x_scr[h, 0:HALO, :] = ahead[:, h * HEAD : (h + 1) * HEAD]
        x_scr[h, HALO:, :] = block.T

    row = lax.broadcasted_iota(jnp.int32, (8, HEAD), 0)

    def head(h, carry):
        lanes = pl.ds(pl.multiple_of(h * HEAD, HEAD), HEAD)
        at_head = pl.ds(h, 1)
        taps = [taps_ref[i : i + 1, lanes] for i in range(4)]
        shifted = {
            off: x_scr[h, pl.ds(HALO + off, 8, stride=SPAN), :] for off in range(-3, SPAN)
        }
        conv = []
        for k in range(SPAN):
            total = taps[0] * shifted[k] + bias_ref[at_head, :]
            for back in range(1, 4):
                valid = mask_ref[back, 8 * k : 8 * k + 8, :]
                total = total + taps[back] * (shifted[k - back] * valid)
            conv.append(total)
        conv = jnp.concatenate(conv, axis=0).astype(BF16)
        gates = jnp.concatenate([gate_a_ref[h], gate_i_ref[h]], axis=1)
        both = jnp.dot(conv, gates, preferred_element_type=F32)
        rgate = jax.nn.sigmoid(both[:, :HEAD] + bias_a_ref[at_head, :])
        igate = jax.nn.sigmoid(both[:, HEAD:] + bias_i_ref[at_head, :])
        logdecay = (-8.0 * rate_ref[at_head, :]) * rgate
        decay = jnp.exp(logdecay)
        same = mask_ref[0]
        twice = 2.0 * logdecay
        series = 1.0 + twice * (
            1 / 2
            + twice
            * (1 / 6 + twice * (1 / 24 + twice * (1 / 120 + twice * (1 / 720 + twice * (1 / 5040)))))
        )
        lost = jnp.where(twice > -0.5, -twice * series, 1.0 - decay * decay)
        factor = jnp.where(same > 0.5, jnp.sqrt(lost), 1.0)
        inflow = factor * igate * conv.astype(F32)
        keep = decay * same
        prods, states = [keep[0:8]], [inflow[0:8]]
        for k in range(1, SPAN):
            part = keep[8 * k : 8 * k + 8]
            prods.append(part * prods[-1])
            states.append(part * states[-1] + inflow[8 * k : 8 * k + 8])
        prod, state = prods[-1], states[-1]
        for by in (1, 2, 4):
            before_prod = jnp.where(row >= by, pltpu.roll(prod, by, 0), 1.0)
            before_state = jnp.where(row >= by, pltpu.roll(state, by, 0), 0.0)
            state = prod * before_state + state
            prod = prod * before_prod
        end_ref[0:1, lanes] = prod[7:8]
        end_ref[1:2, lanes] = state[7:8]
        in_prod = jnp.where(row >= 1, pltpu.roll(prod, 1, 0), 1.0)
        in_state = jnp.where(row >= 1, pltpu.roll(state, 1, 0), 0.0)
        for k in range(SPAN):
            at = pl.ds(k, 8, stride=SPAN)
            gelu = gelu_ref[h, at, :]
            state_ref[h, at, :] = (states[k] + prods[k] * in_state) * gelu
            prod_ref[h, at, :] = (prods[k] * in_prod) * gelu
        return carry

    lax.fori_loop(0, HEADS, head, 0)


def finish_kernel(state_ref, prod_ref, in_ref, out_ref):
    def head(h, carry):
        lanes = pl.ds(pl.multiple_of(h * HEAD, HEAD), HEAD)
        out_ref[:, lanes] = (state_ref[h] + prod_ref[h] * in_ref[:, lanes]).astype(BF16)
        return carry

    lax.fori_loop(0, HEADS, head, 0)


def call(kernel, outs, ins, scratch=(), room=16, flops=0, moved=0):
    return pl.pallas_call(
        kernel,
        out_shape=outs,
        in_specs=ins,
        out_specs=jax.tree.map(lambda _: VMEM, outs),
        scratch_shapes=list(scratch),
        compiler_params=pltpu.CompilerParams(vmem_limit_bytes=room * 2**20),
        cost_estimate=pl.CostEstimate(flops=flops, bytes_accessed=moved, transcendentals=0),
    )


def joined(earlier, later):
    return jnp.concatenate(
        [earlier[:1] * later[:1], later[:1] * earlier[1:] + later[1:]], axis=0
    )


def body(
    tokens,
    gate_input,
    segment_ids,
    in_weight,
    conv_weight,
    conv_bias,
    gate_a,
    gate_i,
    bias_a,
    bias_i,
    decay_rate,
):
    ctx = ("y", "z")
    own = tokens[0]
    at = jnp.stack([lax.axis_index(a) for a in ("x", "c", "y")] + [lax.axis_index(ctx)]).astype(
        jnp.int32
    )

    streams = [own, shift(own, "x", 1), shift(own, "x", -1), shift(own, "x", 2)]
    filled = jnp.pad(in_weight, ((0, 0), (0, 512 - COLS)))
    column = lax.all_to_all(
        jnp.broadcast_to(filled[None], (8,) + filled.shape), "z", 0, 0, tiled=True
    ).reshape(-1, 512)[:, :COLS].T
    from_back = shift(column, "y", 1)
    from_ahead = shift(column, "y", -1)
    near = [column, flip(column), from_back, flip(from_back), from_ahead, flip(from_ahead)]
    first = shift(from_back[:CUT], "y", 1)
    second = shift(from_ahead[CUT:], "y", -1)

    documents = jnp.pad(segment_ids.astype(BF16), ((0, 15), (0, DEPTH - LENGTH)))
    ahead = shift(jnp.concatenate([t[-HALO:] for t in streams] + [documents], axis=0), ctx, 1)

    part, rows_far = call(
        project_kernel,
        (
            jax.ShapeDtypeStruct((2, COLS, ROWS), F32),
            jax.ShapeDtypeStruct((ROWS, 640), BF16),
        ),
        [SMEM] + [ANY] * 5 + [VMEM] * 6,
        [pltpu.VMEM((ROWS, DEPTH), BF16), pltpu.SemaphoreType.DMA((5,))],
        flops=2 * 560 * 1920 * 864,
        moved=9_000_000,
    )(at, *streams, ahead, *near)
    first, second, part = lax.optimization_barrier((first, second, part))
    far = [first, flip(first), second, flip(second)]
    sent = call(
        pack_kernel,
        [jax.ShapeDtypeStruct((2, PACK, 128), BF16)] * 4,
        [SMEM] + [VMEM] * 6,
        [pltpu.VMEM((COLS, 640), BF16), pltpu.VMEM((512, 128), F32)],
        flops=2 * 560 * 640 * 864,
        moved=5_000_000,
    )(at, part, rows_far, *far)
    gelu, masks = call(
        prepare_kernel,
        (
            jax.ShapeDtypeStruct((HEADS, LENGTH, HEAD), F32),
            jax.ShapeDtypeStruct((4, LENGTH, HEAD), F32),
        ),
        [SMEM] + [VMEM] * 3,
        [pltpu.VMEM((LENGTH + HALO, HEAD), F32)],
        moved=2_700_000,
    )(at, gate_input[0], segment_ids, ahead)
    got = [
        sent[0],
        shift(sent[2], "x", 1),
        shift(sent[1], "x", -1),
        shift(sent[3], "x", 2),
    ]
    states, prods, ends = call(
        recur_kernel,
        (
            jax.ShapeDtypeStruct((HEADS, LENGTH, HEAD), F32),
            jax.ShapeDtypeStruct((HEADS, LENGTH, HEAD), F32),
            jax.ShapeDtypeStruct((2, WIDTH), F32),
        ),
        [SMEM] + [ANY] * 4 + [VMEM] * 9,
        [
            pltpu.VMEM((HEADS, LENGTH + HALO, HEAD), F32),
            pltpu.VMEM((8, PACK, 128), BF16),
            pltpu.SemaphoreType.DMA((4,)),
        ],
        flops=2 * 128 * 3456 * 256,
        moved=8_000_000,
    )(
        at,
        *got,
        masks,
        gelu,
        conv_weight,
        *(v.reshape(HEADS, HEAD) for v in (conv_bias, bias_a, bias_i, decay_rate)),
        gate_a,
        gate_i,
    )

    two = joined(shift(ends, ctx, 1), ends)
    pairs = [shift(two, ctx, by) for by in (7, 5, 3, 1)]
    incoming = functools.reduce(joined, pairs)[1:]
    out = call(
        finish_kernel,
        jax.ShapeDtypeStruct((LENGTH, WIDTH), BF16),
        [VMEM] * 3,
        moved=4_400_000,
    )(states, prods, incoming)
    return out[None]


def solution(mesh):
    fine = Mesh(mesh.devices.reshape(4, 8, 4, 2), ("y", "z", "x", "c"))
    ctx, fsdp = ("y", "z"), ("x", "c")
    placed = (
        P(fsdp, ctx, None),
        P(fsdp, ctx, None),
        P(fsdp, ctx),
        P(ctx, fsdp),
        P(),
        P(),
        P(),
        P(),
        P(),
        P(),
        P(),
    )
    return jax.shard_map(
        body, mesh=fine, in_specs=placed, out_specs=P(fsdp, ctx, None), check_vma=False
    )
```

```python
import functools

import jax
import jax.numpy as jnp
from jax import lax
from jax.experimental import pallas as pl
from jax.experimental.pallas import tpu as pltpu
from jax.sharding import Mesh
from jax.sharding import PartitionSpec as P

F32 = jnp.float32
BF16 = jnp.bfloat16
VMEM = pl.BlockSpec(memory_space=pltpu.VMEM)
ANY = pl.BlockSpec(memory_space=pl.ANY)
SMEM = pl.BlockSpec(memory_space=pltpu.SMEM)

LENGTH = 128
WIDTH = 3456
DEPTH = 2560
COLS = 432
HEAD = 128
HEADS = 27
SPAN = 16
HALO = 8
PACK = COLS + 32
CUT = 208
AHEAD = 16
NEAR, FAR = 20, 8
ROWS = 4 * LENGTH + AHEAD


def shift(value, axis, by):
    count = lax.axis_size(axis)
    return lax.ppermute(value, axis, [(i, (i + by) % count) for i in range(count)])


def flip(value):
    return lax.ppermute(value, "c", [(0, 1), (1, 0)])


def prepare_kernel(at_ref, gate_ref, ids_ref, ahead_ref, gelu_ref, mask_ref, ids_scr):
    def head(h, carry):
        lanes = pl.ds(pl.multiple_of(h * HEAD, HEAD), HEAD)
        gelu_ref[h] = jax.nn.gelu(gate_ref[:, lanes].astype(F32), approximate=True)
        return carry

    lax.fori_loop(0, HEADS, head, 0)
    prior = ahead_ref[:, 0:LENGTH].astype(F32)[0:1]
    prior = jnp.where(at_ref[3] == 0, -1.0, prior)
    prior = jnp.broadcast_to(prior, (LENGTH, LENGTH)).T
    own = jnp.broadcast_to(ids_ref[...].astype(F32), (LENGTH, LENGTH)).T
    ids_scr[0:HALO, :] = prior[LENGTH - HALO :, :]
    ids_scr[HALO:, :] = own
    for k in range(SPAN):
        here = ids_scr[pl.ds(HALO + k, 8, stride=SPAN), :]
        for back in range(1, 4):
            there = ids_scr[pl.ds(HALO + k - back, 8, stride=SPAN), :]
            same = (here == there).astype(F32)
            mask_ref[back, 8 * k : 8 * k + 8, :] = same
            if back == 1:
                mask_ref[0, 8 * k : 8 * k + 8, :] = same


def copies(pairs, sems):
    made = [
        pltpu.make_async_copy(src, dst, sems.at[i]) for i, (src, dst) in enumerate(pairs)
    ]
    for copy in made:
        copy.start()
    return made


def across(weight, rows):
    return lax.dot_general(
        weight, rows, (((1,), (1,)), ((), ())), preferred_element_type=F32
    )


def project_kernel(at_ref, t0, t1, t2, t3, ahead, *refs):
    weights, (part_ref, far_ref, rows_ref, sems) = refs[:6], refs[6:]
    y = at_ref[2]
    pairs = [
        (ref, rows_ref.at[pl.ds(i * LENGTH, LENGTH)]) for i, ref in enumerate((t0, t1, t2, t3))
    ] + [(ahead, rows_ref.at[pl.ds(4 * LENGTH, AHEAD)])]
    for copy in copies(pairs, sems):
        copy.wait()
    for half in range(2):
        total = None
        for j, back in enumerate((0, 3, 1)):
            start = pl.multiple_of(lax.rem(y + back, 4) * 640, 128)
            part = across(weights[2 * j + half][...], rows_ref[:, pl.ds(start, 640)])
            total = part if total is None else total + part
        part_ref[half] = total
    far_ref[...] = rows_ref[:, pl.ds(pl.multiple_of(lax.rem(y + 2, 4) * 640, 128), 640)]


def pack_kernel(at_ref, part_ref, far_ref, *refs):
    weights, outs, (all_ref, wide_ref) = refs[:4], refs[4:8], refs[8:]
    c = at_ref[1]
    for half in range(2):
        all_ref[0:CUT, :] = weights[half][...]
        all_ref[CUT:COLS, :] = weights[2 + half][...]
        total = part_ref[half] + across(all_ref[...], far_ref[...])
        place = c if half == 0 else 1 - c
        main = pl.ds(pl.multiple_of(place * COLS, 16), COLS)
        wide_ref[0:COLS, 0:AHEAD] = total[:, 4 * LENGTH :]
        turned = [wide_ref[j * 128 : (j + 1) * 128, :].T for j in range(4)]
        for i, out_ref in enumerate(outs):
            out_ref[main, :] = total[:, i * LENGTH : (i + 1) * LENGTH].astype(BF16)
            group = [t[8 * (i // 2) : 8 * (i // 2) + 8, :] for t in turned]
            if i % 2 == 0:
                group = [pltpu.roll(g, 4, 0) for g in group]
            for j in range(2):
                rest = pl.ds(pl.multiple_of(2 * COLS + 32 * place + 16 * j, 16), 16)
                out_ref[rest, :] = jnp.concatenate(group[2 * j : 2 * j + 2], axis=0).astype(BF16)


def far_head(x):
    return jnp.minimum((lax.rem(x + 2, 4) * HEADS) // 4, HEADS - FAR)


def recur(at_ref, got, refs, far, state_ref, prod_ref, end_ref, scratch):
    (
        mask_ref,
        gelu_ref,
        taps_ref,
        bias_ref,
        bias_a_ref,
        bias_i_ref,
        rate_ref,
        gate_a_ref,
        gate_i_ref,
    ) = refs
    x_scr, main_ref, pack_ref, ahead_ref, sems = scratch
    x = at_ref[0]
    pairs = []
    for back, ref in zip((0, 1, 3, 2), got):
        block = lax.rem(x + 4 - back, 4)
        rows = pl.ds(pl.multiple_of(block * (2 * COLS), 16), 2 * COLS)
        pairs.append((ref.at[pl.ds(0, 2 * COLS)], main_ref.at[rows]))
        pairs.append((ref.at[pl.ds(2 * COLS, 64)], pack_ref.at[block]))
    for copy in copies(pairs, sems):
        copy.wait()
    ahead = []
    for f in range(8):
        packed = pack_ref[f // 2, 32 * (f % 2) : 32 * (f % 2) + 32, :].astype(F32)
        ahead += [packed[8 * j : 8 * j + 8, : min(128, COLS - 128 * j)] for j in range(4)]
    ahead_ref[...] = jnp.concatenate(ahead, axis=1)

    row = lax.broadcasted_iota(jnp.int32, (8, HEAD), 0)
    start = far_head(x)

    def head(i, slot):
        h = start + i if far else lax.rem(start + FAR + i, HEADS)
        out = i if far else h
        lanes = pl.ds(pl.multiple_of(h * HEAD, HEAD), HEAD)
        at_head = pl.ds(h, 1)
        x_scr[slot, 0:HALO, :] = ahead_ref[:, lanes]
        x_scr[slot, HALO:, :] = main_ref[lanes, :].astype(F32).T
        taps = [taps_ref[n : n + 1, lanes] for n in range(4)]
        bias = bias_ref[at_head, :]
        shifted = {
            off: x_scr[slot, pl.ds(HALO + off, 8, stride=SPAN), :] for off in range(-3, SPAN)
        }
        conv = []
        for k in range(SPAN):
            total = taps[0] * shifted[k] + bias
            for back in range(1, 4):
                valid = mask_ref[back, 8 * k : 8 * k + 8, :]
                total = total + taps[back] * (shifted[k - back] * valid)
            conv.append(total)
        conv = jnp.concatenate(conv, axis=0).astype(BF16)
        gates = jnp.concatenate([gate_a_ref[h], gate_i_ref[h]], axis=1)
        both = jnp.dot(conv, gates, preferred_element_type=F32)
        rgate = jax.nn.sigmoid(both[:, :HEAD] + bias_a_ref[at_head, :])
        igate = jax.nn.sigmoid(both[:, HEAD:] + bias_i_ref[at_head, :])
        logdecay = (-8.0 * rate_ref[at_head, :]) * rgate
        decay = jnp.exp(logdecay)
        same = mask_ref[0]
        twice = 2.0 * logdecay
        series = 1.0 + twice * (
            1 / 2
            + twice
            * (1 / 6 + twice * (1 / 24 + twice * (1 / 120 + twice * (1 / 720 + twice * (1 / 5040)))))
        )
        lost = jnp.where(twice > -0.5, -twice * series, 1.0 - decay * decay)
        factor = jnp.where(same > 0.5, jnp.sqrt(lost), 1.0)
        inflow = factor * igate * conv.astype(F32)
        keep = decay * same
        prods, states = [keep[0:8]], [inflow[0:8]]
        for k in range(1, SPAN):
            part = keep[8 * k : 8 * k + 8]
            prods.append(part * prods[-1])
            states.append(part * states[-1] + inflow[8 * k : 8 * k + 8])
        prod, state = prods[-1], states[-1]
        for by in (1, 2, 4):
            before_prod = jnp.where(row >= by, pltpu.roll(prod, by, 0), 1.0)
            before_state = jnp.where(row >= by, pltpu.roll(state, by, 0), 0.0)
            state = prod * before_state + state
            prod = prod * before_prod
        end_ref[0:1, lanes] = prod[7:8]
        end_ref[1:2, lanes] = state[7:8]
        in_prod = jnp.where(row >= 1, pltpu.roll(prod, 1, 0), 1.0)
        in_state = jnp.where(row >= 1, pltpu.roll(state, 1, 0), 0.0)
        for k in range(SPAN):
            at = pl.ds(k, 8, stride=SPAN)
            gelu = gelu_ref[h, at, :]
            state_ref[out, at, :] = (states[k] + prods[k] * in_state) * gelu
            prod_ref[out, at, :] = (prods[k] * in_prod) * gelu

    def pair(i, carry):
        for slot in range(2):
            head(2 * i + slot, slot)
        return carry

    lax.fori_loop(0, (FAR if far else NEAR) // 2, pair, 0)


def near_kernel(at_ref, *refs):
    state_ref, prod_ref, end_ref = refs[12:15]
    recur(at_ref, refs[:3], refs[3:12], False, state_ref, prod_ref, end_ref, refs[15:])


def far_kernel(at_ref, *refs):
    ends_ref = refs[13]
    state_ref, prod_ref, end_ref = refs[14:17]
    end_ref[...] = ends_ref[...]
    recur(at_ref, refs[:4], refs[4:13], True, state_ref, prod_ref, end_ref, refs[17:])


def finish_kernel(at_ref, state_ref, prod_ref, far_state_ref, far_prod_ref, in_ref, out_ref):
    start = far_head(at_ref[0])

    def near(i, carry):
        h = lax.rem(start + FAR + i, HEADS)
        lanes = pl.ds(pl.multiple_of(h * HEAD, HEAD), HEAD)
        out_ref[:, lanes] = (state_ref[h] + prod_ref[h] * in_ref[:, lanes]).astype(BF16)
        return carry

    def far(i, carry):
        lanes = pl.ds(pl.multiple_of((start + i) * HEAD, HEAD), HEAD)
        out_ref[:, lanes] = (far_state_ref[i] + far_prod_ref[i] * in_ref[:, lanes]).astype(BF16)
        return carry

    lax.fori_loop(0, HEADS - FAR, near, 0)
    lax.fori_loop(0, FAR, far, 0)


def call(kernel, outs, ins, scratch=(), room=16, flops=0, moved=0):
    return pl.pallas_call(
        kernel,
        out_shape=outs,
        in_specs=ins,
        out_specs=jax.tree.map(lambda _: VMEM, outs),
        scratch_shapes=list(scratch),
        compiler_params=pltpu.CompilerParams(vmem_limit_bytes=room * 2**20),
        cost_estimate=pl.CostEstimate(flops=flops, bytes_accessed=moved, transcendentals=0),
    )


def joined(earlier, later):
    return jnp.concatenate(
        [earlier[:1] * later[:1], later[:1] * earlier[1:] + later[1:]], axis=0
    )


def body(
    tokens,
    gate_input,
    segment_ids,
    in_weight,
    conv_weight,
    conv_bias,
    gate_a,
    gate_i,
    bias_a,
    bias_i,
    decay_rate,
):
    ctx = ("y", "z")
    own = tokens[0]
    at = jnp.stack([lax.axis_index(a) for a in ("x", "c", "y")] + [lax.axis_index(ctx)]).astype(
        jnp.int32
    )

    copied = jnp.broadcast_to(in_weight[None], (8,) + in_weight.shape)
    column = lax.all_to_all(copied, "z", 0, 0, tiled=True).reshape(-1, COLS).T
    streams = [own, shift(own, "x", 1), shift(own, "x", -1), shift(own, "x", 2)]
    from_back = shift(column, "y", 1)
    from_ahead = shift(column, "y", -1)
    near = [column, flip(column), from_back, flip(from_back), from_ahead, flip(from_ahead)]
    first = shift(from_back[:CUT], "y", 1)
    second = shift(from_ahead[CUT:], "y", -1)

    documents = jnp.pad(segment_ids.astype(BF16), ((0, 0), (0, DEPTH - LENGTH)))
    ahead = shift(
        jnp.concatenate([documents, own[-3:]] + [t[-4:] for t in streams[1:]], axis=0), ctx, 1
    )

    part, rows_far = call(
        project_kernel,
        (
            jax.ShapeDtypeStruct((2, COLS, ROWS), F32),
            jax.ShapeDtypeStruct((ROWS, 640), BF16),
        ),
        [SMEM] + [ANY] * 5 + [VMEM] * 6,
        [pltpu.VMEM((ROWS, DEPTH), BF16), pltpu.SemaphoreType.DMA((5,))],
        flops=2 * 560 * 1920 * 864,
        moved=9_000_000,
    )(at, *streams, ahead, *near)
    first, second, part = lax.optimization_barrier((first, second, part))
    far = [first, flip(first), second, flip(second)]
    sent = call(
        pack_kernel,
        [jax.ShapeDtypeStruct((2 * PACK, 128), BF16)] * 4,
        [SMEM] + [VMEM] * 6,
        [pltpu.VMEM((COLS, 640), BF16), pltpu.VMEM((512, 128), F32)],
        flops=2 * 560 * 640 * 864,
        moved=5_000_000,
    )(at, part, rows_far, *far)
    gelu, masks = call(
        prepare_kernel,
        (
            jax.ShapeDtypeStruct((HEADS, LENGTH, HEAD), F32),
            jax.ShapeDtypeStruct((4, LENGTH, HEAD), F32),
        ),
        [SMEM] + [VMEM] * 3,
        [pltpu.VMEM((LENGTH + HALO, HEAD), F32)],
        moved=2_700_000,
    )(at, gate_input[0], segment_ids, ahead)
    got = [
        sent[0],
        shift(sent[2], "x", 1),
        shift(sent[1], "x", -1),
        shift(sent[3], "x", 2),
    ]
    shared = (
        masks,
        gelu,
        conv_weight,
        *(v.reshape(HEADS, HEAD) for v in (conv_bias, bias_a, bias_i, decay_rate)),
        gate_a,
        gate_i,
    )
    scratch = [
        pltpu.VMEM((2, LENGTH + HALO, HEAD), F32),
        pltpu.VMEM((WIDTH, LENGTH), BF16),
        pltpu.VMEM((4, 64, 128), BF16),
        pltpu.VMEM((HALO, WIDTH), F32),
        pltpu.SemaphoreType.DMA((8,)),
    ]

    def walked(heads):
        return (
            jax.ShapeDtypeStruct((heads, LENGTH, HEAD), F32),
            jax.ShapeDtypeStruct((heads, LENGTH, HEAD), F32),
            jax.ShapeDtypeStruct((2, WIDTH), F32),
        )

    states, prods, ends = call(
        near_kernel,
        walked(HEADS),
        [SMEM] + [ANY] * 3 + [VMEM] * 9,
        scratch,
        flops=2 * 128 * 2560 * 256,
        moved=20_000_000,
    )(at, *got[:3], *shared)
    far_states, far_prods, ends = call(
        far_kernel,
        walked(FAR),
        [SMEM] + [ANY] * 4 + [VMEM] * 10,
        scratch,
        flops=2 * 128 * 1024 * 256,
        moved=8_000_000,
    )(at, *got, *shared, ends)

    two = joined(shift(ends, ctx, 1), ends)
    pairs = [shift(two, ctx, by) for by in (7, 5, 3, 1)]
    incoming = functools.reduce(joined, pairs)[1:]
    out = call(
        finish_kernel,
        jax.ShapeDtypeStruct((LENGTH, WIDTH), BF16),
        [SMEM] + [VMEM] * 5,
        moved=4_400_000,
    )(at, states, prods, far_states, far_prods, incoming)
    return out[None]


def solution(mesh):
    fine = Mesh(mesh.devices.reshape(4, 8, 4, 2), ("y", "z", "x", "c"))
    ctx, fsdp = ("y", "z"), ("x", "c")
    placed = (
        P(fsdp, ctx, None),
        P(fsdp, ctx, None),
        P(fsdp, ctx),
        P(ctx, fsdp),
        P(),
        P(),
        P(),
        P(),
        P(),
        P(),
        P(),
    )
    return jax.shard_map(
        body, mesh=fine, in_specs=placed, out_specs=P(fsdp, ctx, None), check_vma=False
    )
```

```python
import functools

import jax
import jax.numpy as jnp
from jax import lax
from jax.experimental import pallas as pl
from jax.experimental.pallas import tpu as pltpu
from jax.sharding import Mesh
from jax.sharding import PartitionSpec as P

F32 = jnp.float32
BF16 = jnp.bfloat16
VMEM = pl.BlockSpec(memory_space=pltpu.VMEM)
ANY = pl.BlockSpec(memory_space=pl.ANY)
SMEM = pl.BlockSpec(memory_space=pltpu.SMEM)

LENGTH = 128
WIDTH = 3456
DEPTH = 2560
COLS = 432
HEAD = 128
HEADS = 27
SPAN = 16
HALO = 8
PACK = COLS + 32
CUT = 208
AHEAD = 16
SIDE = 4
NEAR, FAR = 20, 8
ROWS = 4 * LENGTH + AHEAD


def shift(value, axis, by):
    count = lax.axis_size(axis)
    return lax.ppermute(value, axis, [(i, (i + by) % count) for i in range(count)])


def flip(value):
    return lax.ppermute(value, "c", [(0, 1), (1, 0)])


def prepare_kernel(at_ref, gate_ref, ids_ref, ahead_ref, gelu_ref, mask_ref, ids_scr):
    def head(h, carry):
        lanes = pl.ds(pl.multiple_of(h * HEAD, HEAD), HEAD)
        gelu_ref[h] = jax.nn.gelu(gate_ref[:, lanes].astype(F32), approximate=True)
        return carry

    lax.fori_loop(0, HEADS, head, 0)
    prior = ahead_ref[:, 0:LENGTH].astype(F32)[0:1]
    prior = jnp.where(at_ref[3] == 0, -1.0, prior)
    prior = jnp.broadcast_to(prior, (LENGTH, LENGTH)).T
    own = jnp.broadcast_to(ids_ref[...].astype(F32), (LENGTH, LENGTH)).T
    ids_scr[0:HALO, :] = prior[LENGTH - HALO :, :]
    ids_scr[HALO:, :] = own
    for k in range(SPAN):
        here = ids_scr[pl.ds(HALO + k, 8, stride=SPAN), :]
        for back in range(1, 4):
            there = ids_scr[pl.ds(HALO + k - back, 8, stride=SPAN), :]
            same = (here == there).astype(F32)
            mask_ref[back, 8 * k : 8 * k + 8, :] = same
            if back == 1:
                mask_ref[0, 8 * k : 8 * k + 8, :] = same


def copies(pairs, sems):
    made = [
        pltpu.make_async_copy(src, dst, sems.at[i]) for i, (src, dst) in enumerate(pairs)
    ]
    for copy in made:
        copy.start()
    return made


def across(weight, rows):
    return lax.dot_general(
        weight, rows, (((1,), (1,)), ((), ())), preferred_element_type=F32
    )


def project_kernel(at_ref, *refs):
    tokens, weights, (part_ref, far_ref, rows_ref, sems) = refs[:12], refs[12:15], refs[15:]
    y = at_ref[2]
    pairs, start = [], 0
    for ref in tokens:
        pairs.append((ref, rows_ref.at[pl.ds(start, ref.shape[0])]))
        start += ref.shape[0]
    for copy in copies(pairs, sems):
        copy.wait()
    for half in range(2):
        total = None
        for w_ref, back in zip(weights, (0, 3, 1)):
            at = pl.ds(pl.multiple_of(lax.rem(y + back, 4) * 640, 128), 640)
            part = across(w_ref[...], rows_ref[half * ROWS : (half + 1) * ROWS, at])
            total = part if total is None else total + part
        part_ref[half] = total
    far_ref[...] = rows_ref[:, pl.ds(pl.multiple_of(lax.rem(y + 2, 4) * 640, 128), 640)]


def pack_kernel(part_ref, far_ref, w0_ref, w1_ref, *refs):
    outs, (all_ref, wide_ref) = refs[:4], refs[4:]
    all_ref[0:CUT, :] = w0_ref[...]
    all_ref[CUT:COLS, :] = w1_ref[...]
    for half in range(2):
        total = part_ref[half] + across(all_ref[...], far_ref[half * ROWS : (half + 1) * ROWS, :])
        wide_ref[0:COLS, 0:AHEAD] = total[:, 4 * LENGTH :]
        turned = [wide_ref[j * 128 : (j + 1) * 128, :].T for j in range(4)]
        top = half * PACK
        for i, out_ref in enumerate(outs):
            out_ref[top : top + COLS, :] = total[:, i * LENGTH : (i + 1) * LENGTH].astype(BF16)
            group = [t[8 * (i // 2) : 8 * (i // 2) + 8, :] for t in turned]
            if i % 2 == 0:
                group = [pltpu.roll(g, 4, 0) for g in group]
            for j in range(2):
                rest = slice(top + COLS + 16 * j, top + COLS + 16 * j + 16)
                out_ref[rest, :] = jnp.concatenate(group[2 * j : 2 * j + 2], axis=0).astype(BF16)


def far_head(x):
    return jnp.minimum((lax.rem(x + 2, 4) * HEADS) // 4, HEADS - FAR)


def recur(at_ref, got, refs, far, state_ref, prod_ref, end_ref, scratch):
    (
        mask_ref,
        gelu_ref,
        taps_ref,
        bias_ref,
        bias_a_ref,
        bias_i_ref,
        rate_ref,
        gate_a_ref,
        gate_i_ref,
    ) = refs
    x_scr, main_ref, pack_ref, ahead_ref, sems = scratch
    x, c = at_ref[0], at_ref[1]
    pairs = []
    for n, ref in enumerate(got):
        place = 2 * lax.rem(x + 4 - (0, 1, 3, 2)[n // 2], 4) + (c if n % 2 == 0 else 1 - c)
        top = (n % 2) * PACK
        rows = pl.ds(pl.multiple_of(place * COLS, 16), COLS)
        pairs.append((ref.at[pl.ds(top, COLS)], main_ref.at[rows]))
        pairs.append((ref.at[pl.ds(top + COLS, 32)], pack_ref.at[place]))
    for copy in copies(pairs, sems):
        copy.wait()
    ahead = []
    for f in range(8):
        packed = pack_ref[f].astype(F32)
        ahead += [packed[8 * j : 8 * j + 8, : min(128, COLS - 128 * j)] for j in range(4)]
    ahead_ref[...] = jnp.concatenate(ahead, axis=1)

    row = lax.broadcasted_iota(jnp.int32, (8, HEAD), 0)
    start = far_head(x)

    def head(i, slot):
        h = start + i if far else lax.rem(start + FAR + i, HEADS)
        out = i if far else h
        lanes = pl.ds(pl.multiple_of(h * HEAD, HEAD), HEAD)
        at_head = pl.ds(h, 1)
        x_scr[slot, 0:HALO, :] = ahead_ref[:, lanes]
        x_scr[slot, HALO:, :] = main_ref[lanes, :].astype(F32).T
        taps = [taps_ref[n : n + 1, lanes] for n in range(4)]
        bias = bias_ref[at_head, :]
        shifted = {
            off: x_scr[slot, pl.ds(HALO + off, 8, stride=SPAN), :] for off in range(-3, SPAN)
        }
        conv = []
        for k in range(SPAN):
            total = taps[0] * shifted[k] + bias
            for back in range(1, 4):
                valid = mask_ref[back, 8 * k : 8 * k + 8, :]
                total = total + taps[back] * (shifted[k - back] * valid)
            conv.append(total)
        conv = jnp.concatenate(conv, axis=0).astype(BF16)
        gates = jnp.concatenate([gate_a_ref[h], gate_i_ref[h]], axis=1)
        both = jnp.dot(conv, gates, preferred_element_type=F32)
        rgate = jax.nn.sigmoid(both[:, :HEAD] + bias_a_ref[at_head, :])
        igate = jax.nn.sigmoid(both[:, HEAD:] + bias_i_ref[at_head, :])
        logdecay = (-8.0 * rate_ref[at_head, :]) * rgate
        decay = jnp.exp(logdecay)
        same = mask_ref[0]
        twice = 2.0 * logdecay
        series = 1.0 + twice * (
            1 / 2
            + twice
            * (1 / 6 + twice * (1 / 24 + twice * (1 / 120 + twice * (1 / 720 + twice * (1 / 5040)))))
        )
        lost = jnp.where(twice > -0.5, -twice * series, 1.0 - decay * decay)
        factor = jnp.where(same > 0.5, jnp.sqrt(lost), 1.0)
        inflow = factor * igate * conv.astype(F32)
        keep = decay * same
        prods, states = [keep[0:8]], [inflow[0:8]]
        for k in range(1, SPAN):
            part = keep[8 * k : 8 * k + 8]
            prods.append(part * prods[-1])
            states.append(part * states[-1] + inflow[8 * k : 8 * k + 8])
        prod, state = prods[-1], states[-1]
        for by in (1, 2, 4):
            before_prod = jnp.where(row >= by, pltpu.roll(prod, by, 0), 1.0)
            before_state = jnp.where(row >= by, pltpu.roll(state, by, 0), 0.0)
            state = prod * before_state + state
            prod = prod * before_prod
        end_ref[0:1, lanes] = prod[7:8]
        end_ref[1:2, lanes] = state[7:8]
        in_prod = jnp.where(row >= 1, pltpu.roll(prod, 1, 0), 1.0)
        in_state = jnp.where(row >= 1, pltpu.roll(state, 1, 0), 0.0)
        for k in range(SPAN):
            at = pl.ds(k, 8, stride=SPAN)
            gelu = gelu_ref[h, at, :]
            state_ref[out, at, :] = (states[k] + prods[k] * in_state) * gelu
            prod_ref[out, at, :] = (prods[k] * in_prod) * gelu

    def several(i, carry):
        for slot in range(SIDE):
            head(SIDE * i + slot, slot)
        return carry

    lax.fori_loop(0, (FAR if far else NEAR) // SIDE, several, 0)


def near_kernel(at_ref, *refs):
    recur(at_ref, refs[:6], refs[6:15], False, *refs[15:18], refs[18:])


def far_kernel(at_ref, *refs):
    refs[20][...] = refs[17][...]
    recur(at_ref, refs[:8], refs[8:17], True, *refs[18:21], refs[21:])


def finish_kernel(at_ref, state_ref, prod_ref, far_state_ref, far_prod_ref, in_ref, out_ref):
    start = far_head(at_ref[0])

    def near(i, carry):
        h = lax.rem(start + FAR + i, HEADS)
        lanes = pl.ds(pl.multiple_of(h * HEAD, HEAD), HEAD)
        out_ref[:, lanes] = (state_ref[h] + prod_ref[h] * in_ref[:, lanes]).astype(BF16)
        return carry

    def far(i, carry):
        lanes = pl.ds(pl.multiple_of((start + i) * HEAD, HEAD), HEAD)
        out_ref[:, lanes] = (far_state_ref[i] + far_prod_ref[i] * in_ref[:, lanes]).astype(BF16)
        return carry

    lax.fori_loop(0, HEADS - FAR, near, 0)
    lax.fori_loop(0, FAR, far, 0)


def call(kernel, outs, ins, scratch=(), room=16, flops=0, moved=0):
    return pl.pallas_call(
        kernel,
        out_shape=outs,
        in_specs=ins,
        out_specs=jax.tree.map(lambda _: VMEM, outs),
        scratch_shapes=list(scratch),
        compiler_params=pltpu.CompilerParams(vmem_limit_bytes=room * 2**20),
        cost_estimate=pl.CostEstimate(flops=flops, bytes_accessed=moved, transcendentals=0),
    )


def joined(earlier, later):
    return jnp.concatenate(
        [earlier[:1] * later[:1], later[:1] * earlier[1:] + later[1:]], axis=0
    )


def body(
    tokens,
    gate_input,
    segment_ids,
    in_weight,
    conv_weight,
    conv_bias,
    gate_a,
    gate_i,
    bias_a,
    bias_i,
    decay_rate,
):
    ctx = ("y", "z")
    own = tokens[0]
    at = jnp.stack([lax.axis_index(a) for a in ("x", "c", "y")] + [lax.axis_index(ctx)]).astype(
        jnp.int32
    )

    copied = jnp.broadcast_to(in_weight[None], (8,) + in_weight.shape)
    column = lax.all_to_all(copied, "z", 0, 0, tiled=True).reshape(-1, COLS).T
    one_back, one_ahead = shift(own, "x", 1), shift(own, "x", -1)
    column, one_back, one_ahead = lax.optimization_barrier((column, one_back, one_ahead))
    upper = shift(one_back[: LENGTH // 2], "x", 1)
    lower = shift(one_ahead[LENGTH // 2 :], "x", -1)
    streams = [own, one_back, one_ahead, upper, lower]
    from_back = shift(column, "y", 1)
    from_ahead = shift(column, "y", -1)
    first = shift(from_back[:CUT], "y", 1)
    second = shift(from_ahead[CUT:], "y", -1)

    documents = jnp.pad(segment_ids.astype(BF16), ((0, 0), (0, DEPTH - LENGTH)))
    ahead = shift(
        jnp.concatenate([documents, own[-3:]] + [t[-4:] for t in (one_back, one_ahead, lower)], axis=0), ctx, 1
    )

    streams.append(ahead)
    streams += [flip(t) for t in streams]
    part, rows_far = call(
        project_kernel,
        (
            jax.ShapeDtypeStruct((2, COLS, ROWS), F32),
            jax.ShapeDtypeStruct((2 * ROWS, 640), BF16),
        ),
        [SMEM] + [ANY] * 12 + [VMEM] * 3,
        [pltpu.VMEM((2 * ROWS, DEPTH), BF16), pltpu.SemaphoreType.DMA((12,))],
        flops=2 * 1056 * 1920 * 432,
        moved=9_000_000,
    )(at, *streams, column, from_back, from_ahead)
    sent = call(
        pack_kernel,
        [jax.ShapeDtypeStruct((2 * PACK, 128), BF16)] * 4,
        [VMEM] * 4,
        [pltpu.VMEM((COLS, 640), BF16), pltpu.VMEM((512, 128), F32)],
        flops=2 * 1056 * 640 * 432,
        moved=5_000_000,
    )(part, rows_far, first, second)
    gelu, masks = call(
        prepare_kernel,
        (
            jax.ShapeDtypeStruct((HEADS, LENGTH, HEAD), F32),
            jax.ShapeDtypeStruct((4, LENGTH, HEAD), F32),
        ),
        [SMEM] + [VMEM] * 3,
        [pltpu.VMEM((LENGTH + HALO, HEAD), F32)],
        moved=2_700_000,
    )(at, gate_input[0], segment_ids, ahead)
    got = [
        sent[0],
        shift(sent[2], "x", 1),
        shift(sent[1], "x", -1),
        shift(sent[3], "x", 2),
    ]
    near = [v for block in got[:3] for v in (block, flip(block))]
    shared = (
        masks,
        gelu,
        conv_weight,
        *(v.reshape(HEADS, HEAD) for v in (conv_bias, bias_a, bias_i, decay_rate)),
        gate_a,
        gate_i,
    )
    scratch = [
        pltpu.VMEM((SIDE, LENGTH + HALO, HEAD), F32),
        pltpu.VMEM((WIDTH, LENGTH), BF16),
        pltpu.VMEM((8, 32, 128), BF16),
        pltpu.VMEM((HALO, WIDTH), F32),
        pltpu.SemaphoreType.DMA((16,)),
    ]

    def walked(heads):
        return (
            jax.ShapeDtypeStruct((heads, LENGTH, HEAD), F32),
            jax.ShapeDtypeStruct((heads, LENGTH, HEAD), F32),
            jax.ShapeDtypeStruct((2, WIDTH), F32),
        )

    states, prods, ends = call(
        near_kernel,
        walked(HEADS),
        [SMEM] + [ANY] * 6 + [VMEM] * 9,
        scratch,
        flops=2 * 128 * 2560 * 256,
        moved=20_000_000,
    )(at, *near, *shared)
    last, ends = lax.optimization_barrier((got[3], ends))
    far_states, far_prods, ends = call(
        far_kernel,
        walked(FAR),
        [SMEM] + [ANY] * 8 + [VMEM] * 10,
        scratch,
        flops=2 * 128 * 1024 * 256,
        moved=8_000_000,
    )(at, *near, last, flip(last), *shared, ends)

    two = joined(shift(ends, ctx, 1), ends)
    pairs = [shift(two, ctx, by) for by in (7, 5, 3, 1)]
    incoming = functools.reduce(joined, pairs)[1:]
    out = call(
        finish_kernel,
        jax.ShapeDtypeStruct((LENGTH, WIDTH), BF16),
        [SMEM] + [VMEM] * 5,
        moved=4_400_000,
    )(at, states, prods, far_states, far_prods, incoming)
    return out[None]


def solution(mesh):
    fine = Mesh(mesh.devices.reshape(4, 8, 4, 2), ("y", "z", "x", "c"))
    ctx, fsdp = ("y", "z"), ("x", "c")
    placed = (
        P(fsdp, ctx, None),
        P(fsdp, ctx, None),
        P(fsdp, ctx),
        P(ctx, fsdp),
        P(),
        P(),
        P(),
        P(),
        P(),
        P(),
        P(),
    )
    return jax.shard_map(
        body, mesh=fine, in_specs=placed, out_specs=P(fsdp, ctx, None), check_vma=False
    )
```

```python
import functools

import jax
import jax.numpy as jnp
from jax import lax
from jax.experimental import pallas as pl
from jax.experimental.pallas import tpu as pltpu
from jax.sharding import Mesh
from jax.sharding import PartitionSpec as P

F32 = jnp.float32
BF16 = jnp.bfloat16
VMEM = pl.BlockSpec(memory_space=pltpu.VMEM)
ANY = pl.BlockSpec(memory_space=pl.ANY)
SMEM = pl.BlockSpec(memory_space=pltpu.SMEM)

LENGTH = 128
WIDTH = 3456
DEPTH = 2560
COLS = 432
HEAD = 128
HEADS = 27
SPAN = 16
HALO = 8
PACK = COLS + 32
CUT = 208
AHEAD = 16
BLOCK = LENGTH + AHEAD
SPLIT = 64
SIDE = 4
NEAR, FAR = 20, 8
ROWS = 4 * BLOCK


def shift(value, axis, by):
    count = lax.axis_size(axis)
    return lax.ppermute(value, axis, [(i, (i + by) % count) for i in range(count)])


def flip(value):
    return lax.ppermute(value, "c", [(0, 1), (1, 0)])


def prepare_kernel(at_ref, gate_ref, ids_ref, ahead_ref, gelu_ref, mask_ref, ids_scr):
    def head(h, carry):
        lanes = pl.ds(pl.multiple_of(h * HEAD, HEAD), HEAD)
        gelu_ref[h] = jax.nn.gelu(gate_ref[:, lanes].astype(F32), approximate=True)
        return carry

    lax.fori_loop(0, HEADS, head, 0)
    prior = ahead_ref[:, 0:LENGTH].astype(F32)[0:1]
    prior = jnp.where(at_ref[3] == 0, -1.0, prior)
    prior = jnp.broadcast_to(prior, (LENGTH, LENGTH)).T
    own = jnp.broadcast_to(ids_ref[...].astype(F32), (LENGTH, LENGTH)).T
    ids_scr[0:HALO, :] = prior[LENGTH - HALO :, :]
    ids_scr[HALO:, :] = own
    for k in range(SPAN):
        here = ids_scr[pl.ds(HALO + k, 8, stride=SPAN), :]
        for back in range(1, 4):
            there = ids_scr[pl.ds(HALO + k - back, 8, stride=SPAN), :]
            same = (here == there).astype(F32)
            mask_ref[back, 8 * k : 8 * k + 8, :] = same
            if back == 1:
                mask_ref[0, 8 * k : 8 * k + 8, :] = same


def copies(pairs, sems):
    made = [
        pltpu.make_async_copy(src, dst, sems.at[i]) for i, (src, dst) in enumerate(pairs)
    ]
    for copy in made:
        copy.start()
    return made


def across(weight, rows):
    return lax.dot_general(
        weight, rows, (((1,), (1,)), ((), ())), preferred_element_type=F32
    )


def project_kernel(at_ref, *refs):
    tokens, weights, (part_ref, far_ref, rows_ref, sems) = refs[:10], refs[10:13], refs[13:]
    y = at_ref[2]
    pairs = []
    for n, ref in enumerate(tokens):
        half, n = n // 5, n % 5
        size = ref.shape[0]
        if n == 3:
            pairs.append((ref, rows_ref.at[pl.ds(half * ROWS + 3 * LENGTH, size)]))
            continue
        top = min(n, 3) * LENGTH + (SPLIT if n == 4 else 0)
        main = size - AHEAD
        pairs.append((ref.at[pl.ds(0, main)], rows_ref.at[pl.ds(half * ROWS + top, main)]))
        rest = half * ROWS + 4 * LENGTH + min(n, 3) * AHEAD
        pairs.append((ref.at[pl.ds(main, AHEAD)], rows_ref.at[pl.ds(rest, AHEAD)]))
    for copy in copies(pairs, sems):
        copy.wait()
    for half in range(2):
        total = None
        for w_ref, back in zip(weights, (0, 3, 1)):
            at = pl.ds(pl.multiple_of(lax.rem(y + back, 4) * 640, 128), 640)
            part = across(w_ref[...], rows_ref[half * ROWS : (half + 1) * ROWS, at])
            total = part if total is None else total + part
        part_ref[half] = total
    far_ref[...] = rows_ref[:, pl.ds(pl.multiple_of(lax.rem(y + 2, 4) * 640, 128), 640)]


def pack_kernel(part_ref, far_ref, w0_ref, w1_ref, *refs):
    outs, (all_ref, wide_ref) = refs[:4], refs[4:]
    all_ref[0:CUT, :] = w0_ref[...]
    all_ref[CUT:COLS, :] = w1_ref[...]
    for half in range(2):
        total = part_ref[half] + across(all_ref[...], far_ref[half * ROWS : (half + 1) * ROWS, :])
        wide_ref[0:COLS, 0 : 4 * AHEAD] = total[:, 4 * LENGTH :]
        turned = [wide_ref[j * 128 : (j + 1) * 128, :].T for j in range(4)]
        top = half * PACK
        for i, out_ref in enumerate(outs):
            out_ref[top : top + COLS, :] = total[:, i * LENGTH : (i + 1) * LENGTH].astype(BF16)
            group = [t[AHEAD * (i + 1) - HALO : AHEAD * (i + 1), :] for t in turned]
            for j in range(2):
                rest = slice(top + COLS + 16 * j, top + COLS + 16 * j + 16)
                out_ref[rest, :] = jnp.concatenate(group[2 * j : 2 * j + 2], axis=0).astype(BF16)


def far_head(x):
    return jnp.minimum((lax.rem(x + 2, 4) * HEADS) // 4, HEADS - FAR)


def recur(at_ref, got, refs, far, state_ref, prod_ref, end_ref, scratch):
    (
        mask_ref,
        gelu_ref,
        taps_ref,
        bias_ref,
        bias_a_ref,
        bias_i_ref,
        rate_ref,
        gate_a_ref,
        gate_i_ref,
    ) = refs
    x_scr, main_ref, pack_ref, ahead_ref, sems = scratch
    x, c = at_ref[0], at_ref[1]
    pairs = []
    for n, ref in enumerate(got):
        place = 2 * lax.rem(x + 4 - (0, 1, 3, 2)[n // 2], 4) + (c if n % 2 == 0 else 1 - c)
        top = (n % 2) * PACK
        rows = pl.ds(pl.multiple_of(place * COLS, 16), COLS)
        pairs.append((ref.at[pl.ds(top, COLS)], main_ref.at[rows]))
        pairs.append((ref.at[pl.ds(top + COLS, 32)], pack_ref.at[place]))
    for copy in copies(pairs, sems):
        copy.wait()
    ahead = []
    for f in range(8):
        packed = pack_ref[f].astype(F32)
        ahead += [packed[8 * j : 8 * j + 8, : min(128, COLS - 128 * j)] for j in range(4)]
    ahead_ref[...] = jnp.concatenate(ahead, axis=1)

    row = lax.broadcasted_iota(jnp.int32, (8, HEAD), 0)
    start = far_head(x)

    def head(i, slot):
        h = start + i if far else lax.rem(start + FAR + i, HEADS)
        out = i if far else h
        lanes = pl.ds(pl.multiple_of(h * HEAD, HEAD), HEAD)
        at_head = pl.ds(h, 1)
        x_scr[slot, 0:HALO, :] = ahead_ref[:, lanes]
        x_scr[slot, HALO:, :] = main_ref[lanes, :].astype(F32).T
        taps = [taps_ref[n : n + 1, lanes] for n in range(4)]
        bias = bias_ref[at_head, :]
        shifted = {
            off: x_scr[slot, pl.ds(HALO + off, 8, stride=SPAN), :] for off in range(-3, SPAN)
        }
        conv = []
        for k in range(SPAN):
            total = taps[0] * shifted[k] + bias
            for back in range(1, 4):
                valid = mask_ref[back, 8 * k : 8 * k + 8, :]
                total = total + taps[back] * (shifted[k - back] * valid)
            conv.append(total)
        conv = jnp.concatenate(conv, axis=0).astype(BF16)
        gates = jnp.concatenate([gate_a_ref[h], gate_i_ref[h]], axis=1)
        both = jnp.dot(conv, gates, preferred_element_type=F32)
        rgate = jax.nn.sigmoid(both[:, :HEAD] + bias_a_ref[at_head, :])
        igate = jax.nn.sigmoid(both[:, HEAD:] + bias_i_ref[at_head, :])
        logdecay = (-8.0 * rate_ref[at_head, :]) * rgate
        decay = jnp.exp(logdecay)
        same = mask_ref[0]
        twice = 2.0 * logdecay
        series = 1.0 + twice * (
            1 / 2
            + twice
            * (1 / 6 + twice * (1 / 24 + twice * (1 / 120 + twice * (1 / 720 + twice * (1 / 5040)))))
        )
        lost = jnp.where(twice > -0.5, -twice * series, 1.0 - decay * decay)
        factor = jnp.where(same > 0.5, jnp.sqrt(lost), 1.0)
        inflow = factor * igate * conv.astype(F32)
        keep = decay * same
        prods, states = [keep[0:8]], [inflow[0:8]]
        for k in range(1, SPAN):
            part = keep[8 * k : 8 * k + 8]
            prods.append(part * prods[-1])
            states.append(part * states[-1] + inflow[8 * k : 8 * k + 8])
        prod, state = prods[-1], states[-1]
        for by in (1, 2, 4):
            before_prod = jnp.where(row >= by, pltpu.roll(prod, by, 0), 1.0)
            before_state = jnp.where(row >= by, pltpu.roll(state, by, 0), 0.0)
            state = prod * before_state + state
            prod = prod * before_prod
        end_ref[0:1, lanes] = prod[7:8]
        end_ref[1:2, lanes] = state[7:8]
        in_prod = jnp.where(row >= 1, pltpu.roll(prod, 1, 0), 1.0)
        in_state = jnp.where(row >= 1, pltpu.roll(state, 1, 0), 0.0)
        for k in range(SPAN):
            at = pl.ds(k, 8, stride=SPAN)
            gelu = gelu_ref[h, at, :]
            state_ref[out, at, :] = (states[k] + prods[k] * in_state) * gelu
            prod_ref[out, at, :] = (prods[k] * in_prod) * gelu

    def several(i, carry):
        for slot in range(SIDE):
            head(SIDE * i + slot, slot)
        return carry

    lax.fori_loop(0, (FAR if far else NEAR) // SIDE, several, 0)


def near_kernel(at_ref, *refs):
    recur(at_ref, refs[:6], refs[6:15], False, *refs[15:18], refs[18:])


def far_kernel(at_ref, *refs):
    refs[20][...] = refs[17][...]
    recur(at_ref, refs[:8], refs[8:17], True, *refs[18:21], refs[21:])


def finish_kernel(at_ref, state_ref, prod_ref, far_state_ref, far_prod_ref, in_ref, out_ref):
    start = far_head(at_ref[0])

    def near(i, carry):
        h = lax.rem(start + FAR + i, HEADS)
        lanes = pl.ds(pl.multiple_of(h * HEAD, HEAD), HEAD)
        out_ref[:, lanes] = (state_ref[h] + prod_ref[h] * in_ref[:, lanes]).astype(BF16)
        return carry

    def far(i, carry):
        lanes = pl.ds(pl.multiple_of((start + i) * HEAD, HEAD), HEAD)
        out_ref[:, lanes] = (far_state_ref[i] + far_prod_ref[i] * in_ref[:, lanes]).astype(BF16)
        return carry

    lax.fori_loop(0, HEADS - FAR, near, 0)
    lax.fori_loop(0, FAR, far, 0)


def call(kernel, outs, ins, scratch=(), room=16, flops=0, moved=0):
    return pl.pallas_call(
        kernel,
        out_shape=outs,
        in_specs=ins,
        out_specs=jax.tree.map(lambda _: VMEM, outs),
        scratch_shapes=list(scratch),
        compiler_params=pltpu.CompilerParams(vmem_limit_bytes=room * 2**20),
        cost_estimate=pl.CostEstimate(flops=flops, bytes_accessed=moved, transcendentals=0),
    )


def joined(earlier, later):
    return jnp.concatenate(
        [earlier[:1] * later[:1], later[:1] * earlier[1:] + later[1:]], axis=0
    )


def body(
    tokens,
    gate_input,
    segment_ids,
    in_weight,
    conv_weight,
    conv_bias,
    gate_a,
    gate_i,
    bias_a,
    bias_i,
    decay_rate,
):
    ctx = ("y", "z")
    own = tokens[0]
    at = jnp.stack([lax.axis_index(a) for a in ("x", "c", "y")] + [lax.axis_index(ctx)]).astype(
        jnp.int32
    )

    documents = jnp.pad(segment_ids.astype(BF16), ((0, 0), (0, DEPTH - LENGTH)))
    last = jnp.concatenate([documents, own[1 - AHEAD :]], axis=0)
    last, weight = lax.optimization_barrier((last, in_weight))
    ahead = shift(last, ctx, 1)
    copied = jnp.broadcast_to(weight[None], (8,) + weight.shape)
    column = lax.all_to_all(copied, "z", 0, 0, tiled=True).reshape(-1, COLS).T
    rows = jnp.concatenate([own, ahead], axis=0)
    one_back, one_ahead = shift(rows, "x", 1), shift(rows, "x", -1)
    column, one_back, one_ahead = lax.optimization_barrier((column, one_back, one_ahead))
    upper = shift(one_back[:SPLIT], "x", 1)
    lower = shift(one_ahead[SPLIT:], "x", -1)
    streams = [rows, one_back, one_ahead, upper, lower]
    from_back = shift(column, "y", 1)
    from_ahead = shift(column, "y", -1)
    from_back, from_ahead = lax.optimization_barrier((from_back, from_ahead))
    first = shift(from_back[:CUT], "y", 1)
    second = shift(from_ahead[CUT:], "y", -1)

    streams += [flip(t) for t in streams]
    part, rows_far = call(
        project_kernel,
        (
            jax.ShapeDtypeStruct((2, COLS, ROWS), F32),
            jax.ShapeDtypeStruct((2 * ROWS, 640), BF16),
        ),
        [SMEM] + [ANY] * 10 + [VMEM] * 3,
        [pltpu.VMEM((2 * ROWS, DEPTH), BF16), pltpu.SemaphoreType.DMA((18,))],
        flops=2 * 1056 * 1920 * 432,
        moved=9_000_000,
    )(at, *streams, column, from_back, from_ahead)
    sent = call(
        pack_kernel,
        [jax.ShapeDtypeStruct((2 * PACK, 128), BF16)] * 4,
        [VMEM] * 4,
        [pltpu.VMEM((COLS, 640), BF16), pltpu.VMEM((512, 128), F32)],
        flops=2 * 1056 * 640 * 432,
        moved=5_000_000,
    )(part, rows_far, first, second)
    gelu, masks = call(
        prepare_kernel,
        (
            jax.ShapeDtypeStruct((HEADS, LENGTH, HEAD), F32),
            jax.ShapeDtypeStruct((4, LENGTH, HEAD), F32),
        ),
        [SMEM] + [VMEM] * 3,
        [pltpu.VMEM((LENGTH + HALO, HEAD), F32)],
        moved=2_700_000,
    )(at, gate_input[0], segment_ids, ahead)
    got = [
        sent[0],
        shift(sent[2], "x", 1),
        shift(sent[1], "x", -1),
        shift(sent[3], "x", 2),
    ]
    near = [v for block in got[:3] for v in (block, flip(block))]
    shared = (
        masks,
        gelu,
        conv_weight,
        *(v.reshape(HEADS, HEAD) for v in (conv_bias, bias_a, bias_i, decay_rate)),
        gate_a,
        gate_i,
    )
    scratch = [
        pltpu.VMEM((SIDE, LENGTH + HALO, HEAD), F32),
        pltpu.VMEM((WIDTH, LENGTH), BF16),
        pltpu.VMEM((8, 32, 128), BF16),
        pltpu.VMEM((HALO, WIDTH), F32),
        pltpu.SemaphoreType.DMA((16,)),
    ]

    def walked(heads):
        return (
            jax.ShapeDtypeStruct((heads, LENGTH, HEAD), F32),
            jax.ShapeDtypeStruct((heads, LENGTH, HEAD), F32),
            jax.ShapeDtypeStruct((2, WIDTH), F32),
        )

    states, prods, ends = call(
        near_kernel,
        walked(HEADS),
        [SMEM] + [ANY] * 6 + [VMEM] * 9,
        scratch,
        flops=2 * 128 * 2560 * 256,
        moved=20_000_000,
    )(at, *near, *shared)
    last, ends = lax.optimization_barrier((got[3], ends))
    far_states, far_prods, ends = call(
        far_kernel,
        walked(FAR),
        [SMEM] + [ANY] * 8 + [VMEM] * 10,
        scratch,
        flops=2 * 128 * 1024 * 256,
        moved=8_000_000,
    )(at, *near, last, flip(last), *shared, ends)

    two = joined(shift(ends, ctx, 1), ends)
    pairs = [shift(two, ctx, by) for by in (7, 5, 3, 1)]
    incoming = functools.reduce(joined, pairs)[1:]
    out = call(
        finish_kernel,
        jax.ShapeDtypeStruct((LENGTH, WIDTH), BF16),
        [SMEM] + [VMEM] * 5,
        moved=4_400_000,
    )(at, states, prods, far_states, far_prods, incoming)
    return out[None]


def solution(mesh):
    fine = Mesh(mesh.devices.reshape(4, 8, 4, 2), ("y", "z", "x", "c"))
    ctx, fsdp = ("y", "z"), ("x", "c")
    placed = (
        P(fsdp, ctx, None),
        P(fsdp, ctx, None),
        P(fsdp, ctx),
        P(ctx, fsdp),
        P(),
        P(),
        P(),
        P(),
        P(),
        P(),
        P(),
    )
    return jax.shard_map(
        body, mesh=fine, in_specs=placed, out_specs=P(fsdp, ctx, None), check_vma=False
    )
```

```python
import functools

import jax
import jax.numpy as jnp
from jax import lax
from jax.experimental import pallas as pl
from jax.experimental.pallas import tpu as pltpu
from jax.sharding import Mesh
from jax.sharding import PartitionSpec as P

F32 = jnp.float32
BF16 = jnp.bfloat16
VMEM = pl.BlockSpec(memory_space=pltpu.VMEM)
ANY = pl.BlockSpec(memory_space=pl.ANY)
HBM = pl.BlockSpec(memory_space=pltpu.HBM)
SMEM = pl.BlockSpec(memory_space=pltpu.SMEM)

LENGTH = 128
WIDTH = 3456
DEPTH = 2560
COLS = 432
HEAD = 128
HEADS = 27
SPAN = 16
HALO = 8
PACK = COLS + 32
CUT = 208
AHEAD = 16
BLOCK = LENGTH + AHEAD
SPLIT = 64
SIDE = 4
NEAR, FAR = 20, 8
ROWS = 4 * BLOCK


def shift(value, axis, by):
    count = lax.axis_size(axis)
    return lax.ppermute(value, axis, [(i, (i + by) % count) for i in range(count)])


def flip(value):
    return lax.ppermute(value, "c", [(0, 1), (1, 0)])


def prepare_kernel(at_ref, gate_ref, ids_ref, ahead_ref, gelu_ref, mask_ref, ids_scr):
    def head(h, carry):
        lanes = pl.ds(pl.multiple_of(h * HEAD, HEAD), HEAD)
        gelu_ref[h] = jax.nn.gelu(gate_ref[:, lanes].astype(F32), approximate=True)
        return carry

    lax.fori_loop(0, HEADS, head, 0)
    prior = ahead_ref[:, 0:LENGTH].astype(F32)[0:1]
    prior = jnp.where(at_ref[3] == 0, -1.0, prior)
    prior = jnp.broadcast_to(prior, (LENGTH, LENGTH)).T
    own = jnp.broadcast_to(ids_ref[...].astype(F32), (LENGTH, LENGTH)).T
    ids_scr[0:HALO, :] = prior[LENGTH - HALO :, :]
    ids_scr[HALO:, :] = own
    for k in range(SPAN):
        here = ids_scr[pl.ds(HALO + k, 8, stride=SPAN), :]
        for back in range(1, 4):
            there = ids_scr[pl.ds(HALO + k - back, 8, stride=SPAN), :]
            same = (here == there).astype(F32)
            mask_ref[back, 8 * k : 8 * k + 8, :] = same
            if back == 1:
                mask_ref[0, 8 * k : 8 * k + 8, :] = same


def copies(pairs, sems):
    made = [
        pltpu.make_async_copy(src, dst, sems.at[i]) for i, (src, dst) in enumerate(pairs)
    ]
    for copy in made:
        copy.start()
    return made


def across(weight, rows):
    return lax.dot_general(
        weight, rows, (((1,), (1,)), ((), ())), preferred_element_type=F32
    )


def project_kernel(at_ref, *refs):
    tokens, weights, (part_ref, far_ref, rows_ref, sems) = refs[:10], refs[10:13], refs[13:]
    y = at_ref[2]
    pairs = []
    for n, ref in enumerate(tokens):
        half, n = n // 5, n % 5
        size = ref.shape[0]
        if n == 3:
            pairs.append((ref, rows_ref.at[pl.ds(half * ROWS + 3 * LENGTH, size)]))
            continue
        top = min(n, 3) * LENGTH + (SPLIT if n == 4 else 0)
        main = size - AHEAD
        pairs.append((ref.at[pl.ds(0, main)], rows_ref.at[pl.ds(half * ROWS + top, main)]))
        rest = half * ROWS + 4 * LENGTH + min(n, 3) * AHEAD
        pairs.append((ref.at[pl.ds(main, AHEAD)], rows_ref.at[pl.ds(rest, AHEAD)]))
    made = copies(pairs, sems)
    far = pl.ds(pl.multiple_of(lax.rem(y + 2, 4) * 640, 128), 640)
    for half in range(2):
        for copy in made[9 * half : 9 * half + 9]:
            copy.wait()
        mine = slice(half * ROWS, (half + 1) * ROWS)
        total = None
        for w_ref, back in zip(weights, (0, 3, 1)):
            at = pl.ds(pl.multiple_of(lax.rem(y + back, 4) * 640, 128), 640)
            part = across(w_ref[...], rows_ref[mine, at])
            total = part if total is None else total + part
        part_ref[half] = total
        far_ref[mine, :] = rows_ref[mine, far]


def pack_kernel(part_ref, far_ref, w0_ref, w1_ref, *refs):
    outs, (all_ref, wide_ref) = refs[:4], refs[4:]
    all_ref[0:CUT, :] = w0_ref[...]
    all_ref[CUT:COLS, :] = w1_ref[...]
    for half in range(2):
        total = part_ref[half] + across(all_ref[...], far_ref[half * ROWS : (half + 1) * ROWS, :])
        wide_ref[0:COLS, 0 : 4 * AHEAD] = total[:, 4 * LENGTH :]
        turned = [wide_ref[j * 128 : (j + 1) * 128, :].T for j in range(4)]
        top = half * PACK
        for i, out_ref in enumerate(outs):
            out_ref[top : top + COLS, :] = total[:, i * LENGTH : (i + 1) * LENGTH].astype(BF16)
            group = [t[AHEAD * (i + 1) - HALO : AHEAD * (i + 1), :] for t in turned]
            for j in range(2):
                rest = slice(top + COLS + 16 * j, top + COLS + 16 * j + 16)
                out_ref[rest, :] = jnp.concatenate(group[2 * j : 2 * j + 2], axis=0).astype(BF16)


def far_head(x):
    return jnp.minimum((lax.rem(x + 2, 4) * HEADS) // 4, HEADS - FAR)


def recur(at_ref, got, refs, far, state_ref, prod_ref, end_ref, scratch):
    (
        mask_ref,
        gelu_ref,
        taps_ref,
        bias_ref,
        bias_a_ref,
        bias_i_ref,
        rate_ref,
        gate_a_ref,
        gate_i_ref,
    ) = refs
    x_scr, main_ref, pack_ref, ahead_ref, sems = scratch
    x, c = at_ref[0], at_ref[1]
    pairs = []
    for n, ref in enumerate(got):
        place = 2 * lax.rem(x + 4 - (0, 1, 3, 2)[n // 2], 4) + (c if n % 2 == 0 else 1 - c)
        top = (n % 2) * PACK
        rows = pl.ds(pl.multiple_of(place * COLS, 16), COLS)
        pairs.append((ref.at[pl.ds(top, COLS)], main_ref.at[rows]))
        pairs.append((ref.at[pl.ds(top + COLS, 32)], pack_ref.at[place]))
    for copy in copies(pairs, sems):
        copy.wait()
    ahead = []
    for f in range(8):
        packed = pack_ref[f].astype(F32)
        ahead += [packed[8 * j : 8 * j + 8, : min(128, COLS - 128 * j)] for j in range(4)]
    ahead_ref[...] = jnp.concatenate(ahead, axis=1)

    row = lax.broadcasted_iota(jnp.int32, (8, HEAD), 0)
    start = far_head(x)

    def head(i, slot):
        h = start + i if far else lax.rem(start + FAR + i, HEADS)
        out = i if far else h
        lanes = pl.ds(pl.multiple_of(h * HEAD, HEAD), HEAD)
        at_head = pl.ds(h, 1)
        x_scr[slot, 0:HALO, :] = ahead_ref[:, lanes]
        x_scr[slot, HALO:, :] = main_ref[lanes, :].astype(F32).T
        taps = [taps_ref[n : n + 1, lanes] for n in range(4)]
        bias = bias_ref[at_head, :]
        shifted = {
            off: x_scr[slot, pl.ds(HALO + off, 8, stride=SPAN), :] for off in range(-3, SPAN)
        }
        conv = []
        for k in range(SPAN):
            total = taps[0] * shifted[k] + bias
            for back in range(1, 4):
                valid = mask_ref[back, 8 * k : 8 * k + 8, :]
                total = total + taps[back] * (shifted[k - back] * valid)
            conv.append(total)
        conv = jnp.concatenate(conv, axis=0).astype(BF16)
        gates = jnp.concatenate([gate_a_ref[h], gate_i_ref[h]], axis=1)
        both = jnp.dot(conv, gates, preferred_element_type=F32)
        rgate = jax.nn.sigmoid(both[:, :HEAD] + bias_a_ref[at_head, :])
        igate = jax.nn.sigmoid(both[:, HEAD:] + bias_i_ref[at_head, :])
        logdecay = (-8.0 * rate_ref[at_head, :]) * rgate
        decay = jnp.exp(logdecay)
        same = mask_ref[0]
        twice = 2.0 * logdecay
        series = 1.0 + twice * (
            1 / 2
            + twice
            * (1 / 6 + twice * (1 / 24 + twice * (1 / 120 + twice * (1 / 720 + twice * (1 / 5040)))))
        )
        lost = jnp.where(twice > -0.5, -twice * series, 1.0 - decay * decay)
        factor = jnp.where(same > 0.5, jnp.sqrt(lost), 1.0)
        inflow = factor * igate * conv.astype(F32)
        keep = decay * same
        prods, states = [keep[0:8]], [inflow[0:8]]
        for k in range(1, SPAN):
            part = keep[8 * k : 8 * k + 8]
            prods.append(part * prods[-1])
            states.append(part * states[-1] + inflow[8 * k : 8 * k + 8])
        prod, state = prods[-1], states[-1]
        for by in (1, 2, 4):
            before_prod = jnp.where(row >= by, pltpu.roll(prod, by, 0), 1.0)
            before_state = jnp.where(row >= by, pltpu.roll(state, by, 0), 0.0)
            state = prod * before_state + state
            prod = prod * before_prod
        end_ref[0:1, lanes] = prod[7:8]
        end_ref[1:2, lanes] = state[7:8]
        in_prod = jnp.where(row >= 1, pltpu.roll(prod, 1, 0), 1.0)
        in_state = jnp.where(row >= 1, pltpu.roll(state, 1, 0), 0.0)
        for k in range(SPAN):
            at = pl.ds(k, 8, stride=SPAN)
            gelu = gelu_ref[h, at, :]
            state_ref[out, at, :] = (states[k] + prods[k] * in_state) * gelu
            prod_ref[out, at, :] = (prods[k] * in_prod) * gelu

    def several(i, carry):
        for slot in range(SIDE):
            head(SIDE * i + slot, slot)
        return carry

    lax.fori_loop(0, (FAR if far else NEAR) // SIDE, several, 0)


def near_kernel(at_ref, *refs):
    recur(at_ref, refs[:6], refs[6:15], False, *refs[15:18], refs[18:])


def far_kernel(at_ref, *refs):
    refs[20][...] = refs[17][...]
    recur(at_ref, refs[:8], refs[8:17], True, *refs[18:21], refs[21:])


def finish_kernel(at_ref, state_ref, prod_ref, far_state_ref, far_prod_ref, in_ref, out_ref):
    start = far_head(at_ref[0])

    def near(i, carry):
        for side in range(4):
            h = lax.rem(start + FAR + 4 * i + side, HEADS)
            lanes = pl.ds(pl.multiple_of(h * HEAD, HEAD), HEAD)
            out_ref[:, lanes] = (state_ref[h] + prod_ref[h] * in_ref[:, lanes]).astype(BF16)
        return carry

    def far(i, carry):
        for side in range(4):
            n = 4 * i + side
            lanes = pl.ds(pl.multiple_of((start + n) * HEAD, HEAD), HEAD)
            out_ref[:, lanes] = (far_state_ref[n] + far_prod_ref[n] * in_ref[:, lanes]).astype(
                BF16
            )
        return carry

    lax.fori_loop(0, NEAR // 4, near, 0)
    lax.fori_loop(0, FAR // 4, far, 0)


def call(kernel, outs, ins, scratch=(), room=16, flops=0, moved=0):
    return pl.pallas_call(
        kernel,
        out_shape=outs,
        in_specs=ins,
        out_specs=jax.tree.map(lambda _: VMEM, outs),
        scratch_shapes=list(scratch),
        compiler_params=pltpu.CompilerParams(vmem_limit_bytes=room * 2**20),
        cost_estimate=pl.CostEstimate(flops=flops, bytes_accessed=moved, transcendentals=0),
    )


def joined(earlier, later):
    return jnp.concatenate(
        [earlier[:1] * later[:1], later[:1] * earlier[1:] + later[1:]], axis=0
    )


def body(
    tokens,
    gate_input,
    segment_ids,
    in_weight,
    conv_weight,
    conv_bias,
    gate_a,
    gate_i,
    bias_a,
    bias_i,
    decay_rate,
):
    ctx = ("y", "z")
    own = tokens[0]
    at = jnp.stack([lax.axis_index(a) for a in ("x", "c", "y")] + [lax.axis_index(ctx)]).astype(
        jnp.int32
    )

    documents = jnp.pad(segment_ids.astype(BF16), ((0, 0), (0, DEPTH - LENGTH)))
    last = jnp.concatenate([documents, own[1 - AHEAD :]], axis=0)
    last, weight = lax.optimization_barrier((last, in_weight))
    ahead = shift(last, ctx, 1)
    copied = jnp.broadcast_to(weight[None], (8,) + weight.shape)
    column = lax.all_to_all(copied, "z", 0, 0, tiled=True).reshape(-1, COLS).T
    rows = jnp.concatenate([own, ahead], axis=0)
    one_back, one_ahead = shift(rows, "x", 1), shift(rows, "x", -1)
    gelu, masks = call(
        prepare_kernel,
        (
            jax.ShapeDtypeStruct((HEADS, LENGTH, HEAD), F32),
            jax.ShapeDtypeStruct((4, LENGTH, HEAD), F32),
        ),
        [SMEM] + [VMEM] * 3,
        [pltpu.VMEM((LENGTH + HALO, HEAD), F32)],
        moved=2_700_000,
    )(at, gate_input[0], segment_ids, ahead)
    column, one_back, one_ahead, gelu, masks = lax.optimization_barrier((column, one_back, one_ahead, gelu, masks))
    upper = shift(one_back[:SPLIT], "x", 1)
    lower = shift(one_ahead[SPLIT:], "x", -1)
    streams = [rows, one_back, one_ahead, upper, lower]
    from_back = shift(column, "y", 1)
    from_ahead = shift(column, "y", -1)
    from_back, from_ahead = lax.optimization_barrier((from_back, from_ahead))
    first = shift(from_back[:CUT], "y", 1)
    second = shift(from_ahead[CUT:], "y", -1)

    streams += [flip(t) for t in streams]
    part, rows_far = call(
        project_kernel,
        (
            jax.ShapeDtypeStruct((2, COLS, ROWS), F32),
            jax.ShapeDtypeStruct((2 * ROWS, 640), BF16),
        ),
        [SMEM] + [ANY] * 5 + [HBM] * 5 + [VMEM] * 3,
        [pltpu.VMEM((2 * ROWS, DEPTH), BF16), pltpu.SemaphoreType.DMA((18,))],
        flops=2 * 1056 * 1920 * 432,
        moved=9_000_000,
    )(at, *streams, column, from_back, from_ahead)
    sent = call(
        pack_kernel,
        [jax.ShapeDtypeStruct((2 * PACK, 128), BF16)] * 4,
        [VMEM] * 4,
        [pltpu.VMEM((COLS, 640), BF16), pltpu.VMEM((512, 128), F32)],
        flops=2 * 1056 * 640 * 432,
        moved=5_000_000,
    )(part, rows_far, first, second)
    got = [
        sent[0],
        shift(sent[2], "x", 1),
        shift(sent[1], "x", -1),
        shift(sent[3], "x", 2),
    ]
    near = [v for block in got[:3] for v in (block, flip(block))]
    shared = (
        masks,
        gelu,
        conv_weight,
        *(v.reshape(HEADS, HEAD) for v in (conv_bias, bias_a, bias_i, decay_rate)),
        gate_a,
        gate_i,
    )
    scratch = [
        pltpu.VMEM((SIDE, LENGTH + HALO, HEAD), F32),
        pltpu.VMEM((WIDTH, LENGTH), BF16),
        pltpu.VMEM((8, 32, 128), BF16),
        pltpu.VMEM((HALO, WIDTH), F32),
        pltpu.SemaphoreType.DMA((16,)),
    ]

    def walked(heads):
        return (
            jax.ShapeDtypeStruct((heads, LENGTH, HEAD), F32),
            jax.ShapeDtypeStruct((heads, LENGTH, HEAD), F32),
            jax.ShapeDtypeStruct((2, WIDTH), F32),
        )

    states, prods, ends = call(
        near_kernel,
        walked(HEADS),
        [SMEM] + [ANY] * 6 + [VMEM] * 9,
        scratch,
        flops=2 * 128 * 2560 * 256,
        moved=20_000_000,
    )(at, *near, *shared)
    last, ends = lax.optimization_barrier((got[3], ends))
    far_states, far_prods, ends = call(
        far_kernel,
        walked(FAR),
        [SMEM] + [ANY] * 8 + [VMEM] * 10,
        scratch,
        flops=2 * 128 * 1024 * 256,
        moved=8_000_000,
    )(at, *near, last, flip(last), *shared, ends)

    two = joined(shift(ends, ctx, 1), ends)
    pairs = [shift(two, ctx, by) for by in (7, 5, 3, 1)]
    incoming = functools.reduce(joined, pairs)[1:]
    out = call(
        finish_kernel,
        jax.ShapeDtypeStruct((LENGTH, WIDTH), BF16),
        [SMEM] + [VMEM] * 5,
        moved=4_400_000,
    )(at, states, prods, far_states, far_prods, incoming)
    return out[None]


def solution(mesh):
    fine = Mesh(mesh.devices.reshape(4, 8, 4, 2), ("y", "z", "x", "c"))
    ctx, fsdp = ("y", "z"), ("x", "c")
    placed = (
        P(fsdp, ctx, None),
        P(fsdp, ctx, None),
        P(fsdp, ctx),
        P(ctx, fsdp),
        P(),
        P(),
        P(),
        P(),
        P(),
        P(),
        P(),
    )
    return jax.shard_map(
        body, mesh=fine, in_specs=placed, out_specs=P(fsdp, ctx, None), check_vma=False
    )
```

```python
import functools

import jax
import jax.numpy as jnp
from jax import lax
from jax.experimental import pallas as pl
from jax.experimental.pallas import tpu as pltpu
from jax.sharding import Mesh
from jax.sharding import PartitionSpec as P

F32 = jnp.float32
BF16 = jnp.bfloat16
VMEM = pl.BlockSpec(memory_space=pltpu.VMEM)
ANY = pl.BlockSpec(memory_space=pl.ANY)
SMEM = pl.BlockSpec(memory_space=pltpu.SMEM)

LENGTH = 128
WIDTH = 3456
DEPTH = 2560
COLS = 432
HEAD = 128
HEADS = 27
SPAN = 16
HALO = 8
PACK = COLS + 32
CUT = 208
AHEAD = 16
BLOCK = LENGTH + AHEAD
SPLIT = 64
SIDE = 4
NEAR, FAR = 20, 8
ROWS = 4 * BLOCK


def shift(value, axis, by):
    count = lax.axis_size(axis)
    return lax.ppermute(value, axis, [(i, (i + by) % count) for i in range(count)])


def flip(value):
    return lax.ppermute(value, "c", [(0, 1), (1, 0)])


def prepare_kernel(at_ref, gate_ref, ids_ref, ahead_ref, gelu_ref, mask_ref, ids_scr):
    def head(h, carry):
        lanes = pl.ds(pl.multiple_of(h * HEAD, HEAD), HEAD)
        gelu_ref[h] = jax.nn.gelu(gate_ref[:, lanes].astype(F32), approximate=True)
        return carry

    lax.fori_loop(0, HEADS, head, 0)
    prior = ahead_ref[:, 0:LENGTH].astype(F32)[0:1]
    prior = jnp.where(at_ref[3] == 0, -1.0, prior)
    prior = jnp.broadcast_to(prior, (LENGTH, LENGTH)).T
    own = jnp.broadcast_to(ids_ref[...].astype(F32), (LENGTH, LENGTH)).T
    ids_scr[0:HALO, :] = prior[LENGTH - HALO :, :]
    ids_scr[HALO:, :] = own
    for k in range(SPAN):
        here = ids_scr[pl.ds(HALO + k, 8, stride=SPAN), :]
        for back in range(1, 4):
            there = ids_scr[pl.ds(HALO + k - back, 8, stride=SPAN), :]
            same = (here == there).astype(F32)
            mask_ref[back, 8 * k : 8 * k + 8, :] = same
            if back == 1:
                mask_ref[0, 8 * k : 8 * k + 8, :] = same


def copies(pairs, sems):
    made = [
        pltpu.make_async_copy(src, dst, sems.at[i]) for i, (src, dst) in enumerate(pairs)
    ]
    for copy in made:
        copy.start()
    return made


def across(weight, rows):
    return lax.dot_general(
        weight, rows, (((1,), (1,)), ((), ())), preferred_element_type=F32
    )


def project_kernel(at_ref, *refs):
    tokens, weights, (part_ref, far_ref) = refs[:10], refs[10:13], refs[13:]
    y = at_ref[2]

    def rows_of(half, at):
        t0, t1, t2, t3, t4 = tokens[5 * half : 5 * half + 5]
        main = [t[0:LENGTH, at] for t in (t0, t1, t2)] + [t3[:, at], t4[0:SPLIT, at]]
        rest = [t[LENGTH:BLOCK, at] for t in (t0, t1, t2)] + [t4[SPLIT:, at]]
        return jnp.concatenate(main + rest, axis=0)

    far = pl.ds(pl.multiple_of(lax.rem(y + 2, 4) * 640, 128), 640)
    for half in range(2):
        total = None
        for w_ref, back in zip(weights, (0, 3, 1)):
            at = pl.ds(pl.multiple_of(lax.rem(y + back, 4) * 640, 128), 640)
            part = across(w_ref[...], rows_of(half, at))
            total = part if total is None else total + part
        part_ref[half] = total
        far_ref[half * ROWS : (half + 1) * ROWS, :] = rows_of(half, far)


def pack_kernel(part_ref, far_ref, w0_ref, w1_ref, *refs):
    outs, (all_ref, wide_ref) = refs[:4], refs[4:]
    all_ref[0:CUT, :] = w0_ref[...]
    all_ref[CUT:COLS, :] = w1_ref[...]
    for half in range(2):
        total = part_ref[half] + across(all_ref[...], far_ref[half * ROWS : (half + 1) * ROWS, :])
        wide_ref[0:COLS, 0 : 4 * AHEAD] = total[:, 4 * LENGTH :]
        turned = [wide_ref[j * 128 : (j + 1) * 128, :].T for j in range(4)]
        top = half * PACK
        for i, out_ref in enumerate(outs):
            out_ref[top : top + COLS, :] = total[:, i * LENGTH : (i + 1) * LENGTH].astype(BF16)
            group = [t[AHEAD * (i + 1) - HALO : AHEAD * (i + 1), :] for t in turned]
            for j in range(2):
                rest = slice(top + COLS + 16 * j, top + COLS + 16 * j + 16)
                out_ref[rest, :] = jnp.concatenate(group[2 * j : 2 * j + 2], axis=0).astype(BF16)


def far_head(x):
    return jnp.minimum((lax.rem(x + 2, 4) * HEADS) // 4, HEADS - FAR)


def recur(at_ref, got, refs, far, state_ref, prod_ref, end_ref, scratch):
    (
        mask_ref,
        gelu_ref,
        taps_ref,
        bias_ref,
        bias_a_ref,
        bias_i_ref,
        rate_ref,
        gate_a_ref,
        gate_i_ref,
    ) = refs
    x_scr, main_ref, pack_ref, ahead_ref, sems = scratch
    x, c = at_ref[0], at_ref[1]
    pairs = []
    for n, ref in enumerate(got):
        place = 2 * lax.rem(x + 4 - (0, 1, 3, 2)[n // 2], 4) + (c if n % 2 == 0 else 1 - c)
        top = (n % 2) * PACK
        rows = pl.ds(pl.multiple_of(place * COLS, 16), COLS)
        pairs.append((ref.at[pl.ds(top, COLS)], main_ref.at[rows]))
        pairs.append((ref.at[pl.ds(top + COLS, 32)], pack_ref.at[place]))
    for copy in copies(pairs, sems):
        copy.wait()
    ahead = []
    for f in range(8):
        packed = pack_ref[f].astype(F32)
        ahead += [packed[8 * j : 8 * j + 8, : min(128, COLS - 128 * j)] for j in range(4)]
    ahead_ref[...] = jnp.concatenate(ahead, axis=1)

    row = lax.broadcasted_iota(jnp.int32, (8, HEAD), 0)
    start = far_head(x)

    def head(i, slot):
        h = start + i if far else lax.rem(start + FAR + i, HEADS)
        out = i if far else h
        lanes = pl.ds(pl.multiple_of(h * HEAD, HEAD), HEAD)
        at_head = pl.ds(h, 1)
        x_scr[slot, 0:HALO, :] = ahead_ref[:, lanes]
        x_scr[slot, HALO:, :] = main_ref[lanes, :].astype(F32).T
        taps = [taps_ref[n : n + 1, lanes] for n in range(4)]
        bias = bias_ref[at_head, :]
        shifted = {
            off: x_scr[slot, pl.ds(HALO + off, 8, stride=SPAN), :] for off in range(-3, SPAN)
        }
        conv = []
        for k in range(SPAN):
            total = taps[0] * shifted[k] + bias
            for back in range(1, 4):
                valid = mask_ref[back, 8 * k : 8 * k + 8, :]
                total = total + taps[back] * (shifted[k - back] * valid)
            conv.append(total)
        conv = jnp.concatenate(conv, axis=0).astype(BF16)
        gates = jnp.concatenate([gate_a_ref[h], gate_i_ref[h]], axis=1)
        both = jnp.dot(conv, gates, preferred_element_type=F32)
        rgate = jax.nn.sigmoid(both[:, :HEAD] + bias_a_ref[at_head, :])
        igate = jax.nn.sigmoid(both[:, HEAD:] + bias_i_ref[at_head, :])
        logdecay = (-8.0 * rate_ref[at_head, :]) * rgate
        decay = jnp.exp(logdecay)
        same = mask_ref[0]
        twice = 2.0 * logdecay
        series = 1.0 + twice * (
            1 / 2
            + twice
            * (1 / 6 + twice * (1 / 24 + twice * (1 / 120 + twice * (1 / 720 + twice * (1 / 5040)))))
        )
        lost = jnp.where(twice > -0.5, -twice * series, 1.0 - decay * decay)
        factor = jnp.where(same > 0.5, jnp.sqrt(lost), 1.0)
        inflow = factor * igate * conv.astype(F32)
        keep = decay * same
        prods, states = [keep[0:8]], [inflow[0:8]]
        for k in range(1, SPAN):
            part = keep[8 * k : 8 * k + 8]
            prods.append(part * prods[-1])
            states.append(part * states[-1] + inflow[8 * k : 8 * k + 8])
        prod, state = prods[-1], states[-1]
        for by in (1, 2, 4):
            before_prod = jnp.where(row >= by, pltpu.roll(prod, by, 0), 1.0)
            before_state = jnp.where(row >= by, pltpu.roll(state, by, 0), 0.0)
            state = prod * before_state + state
            prod = prod * before_prod
        end_ref[0:1, lanes] = prod[7:8]
        end_ref[1:2, lanes] = state[7:8]
        in_prod = jnp.where(row >= 1, pltpu.roll(prod, 1, 0), 1.0)
        in_state = jnp.where(row >= 1, pltpu.roll(state, 1, 0), 0.0)
        for k in range(SPAN):
            at = pl.ds(k, 8, stride=SPAN)
            gelu = gelu_ref[h, at, :]
            state_ref[out, at, :] = (states[k] + prods[k] * in_state) * gelu
            prod_ref[out, at, :] = (prods[k] * in_prod) * gelu

    def several(i, carry):
        for slot in range(SIDE):
            head(SIDE * i + slot, slot)
        return carry

    lax.fori_loop(0, (FAR if far else NEAR) // SIDE, several, 0)


def near_kernel(at_ref, *refs):
    recur(at_ref, refs[:6], refs[6:15], False, *refs[15:18], refs[18:])


def far_kernel(at_ref, *refs):
    refs[20][...] = refs[17][...]
    recur(at_ref, refs[:8], refs[8:17], True, *refs[18:21], refs[21:])


def finish_kernel(at_ref, state_ref, prod_ref, far_state_ref, far_prod_ref, in_ref, out_ref):
    start = far_head(at_ref[0])

    def near(i, carry):
        for side in range(4):
            h = lax.rem(start + FAR + 4 * i + side, HEADS)
            lanes = pl.ds(pl.multiple_of(h * HEAD, HEAD), HEAD)
            out_ref[:, lanes] = (state_ref[h] + prod_ref[h] * in_ref[:, lanes]).astype(BF16)
        return carry

    def far(i, carry):
        for side in range(4):
            n = 4 * i + side
            lanes = pl.ds(pl.multiple_of((start + n) * HEAD, HEAD), HEAD)
            out_ref[:, lanes] = (far_state_ref[n] + far_prod_ref[n] * in_ref[:, lanes]).astype(
                BF16
            )
        return carry

    lax.fori_loop(0, NEAR // 4, near, 0)
    lax.fori_loop(0, FAR // 4, far, 0)


def call(kernel, outs, ins, scratch=(), room=16, flops=0, moved=0):
    return pl.pallas_call(
        kernel,
        out_shape=outs,
        in_specs=ins,
        out_specs=jax.tree.map(lambda _: VMEM, outs),
        scratch_shapes=list(scratch),
        compiler_params=pltpu.CompilerParams(vmem_limit_bytes=room * 2**20),
        cost_estimate=pl.CostEstimate(flops=flops, bytes_accessed=moved, transcendentals=0),
    )


def joined(earlier, later):
    return jnp.concatenate(
        [earlier[:1] * later[:1], later[:1] * earlier[1:] + later[1:]], axis=0
    )


def body(
    tokens,
    gate_input,
    segment_ids,
    in_weight,
    conv_weight,
    conv_bias,
    gate_a,
    gate_i,
    bias_a,
    bias_i,
    decay_rate,
):
    ctx = ("y", "z")
    own = tokens[0]
    at = jnp.stack([lax.axis_index(a) for a in ("x", "c", "y")] + [lax.axis_index(ctx)]).astype(
        jnp.int32
    )

    documents = jnp.pad(segment_ids.astype(BF16), ((0, 0), (0, DEPTH - LENGTH)))
    last = jnp.concatenate([documents, own[1 - AHEAD :]], axis=0)
    last, weight = lax.optimization_barrier((last, in_weight))
    ahead = shift(last, ctx, 1)
    copied = jnp.broadcast_to(weight[None], (8,) + weight.shape)
    column = lax.all_to_all(copied, "z", 0, 0, tiled=True).reshape(-1, COLS).T
    rows = jnp.concatenate([own, ahead], axis=0)
    one_back, one_ahead = shift(rows, "x", 1), shift(rows, "x", -1)
    gelu, masks = call(
        prepare_kernel,
        (
            jax.ShapeDtypeStruct((HEADS, LENGTH, HEAD), F32),
            jax.ShapeDtypeStruct((4, LENGTH, HEAD), F32),
        ),
        [SMEM] + [VMEM] * 3,
        [pltpu.VMEM((LENGTH + HALO, HEAD), F32)],
        room=6,
        moved=2_700_000,
    )(at, gate_input[0], segment_ids, ahead)
    column, one_back, one_ahead = lax.optimization_barrier((column, one_back, one_ahead))
    one_back, gelu, masks = lax.optimization_barrier((one_back, gelu, masks))
    upper = shift(one_back[:SPLIT], "x", 1)
    lower = shift(one_ahead[SPLIT:], "x", -1)
    streams = [rows, one_back, one_ahead, upper, lower]
    from_back = shift(column, "y", 1)
    from_ahead = shift(column, "y", -1)
    from_back, from_ahead = lax.optimization_barrier((from_back, from_ahead))
    first = shift(from_back[:CUT], "y", 1)
    second = shift(from_ahead[CUT:], "y", -1)

    streams += [flip(t) for t in streams]
    part, rows_far = call(
        project_kernel,
        (
            jax.ShapeDtypeStruct((2, COLS, ROWS), F32),
            jax.ShapeDtypeStruct((2 * ROWS, 640), BF16),
        ),
        [SMEM] + [VMEM] * 13,
        flops=2 * 1056 * 1920 * 432,
        moved=9_000_000,
    )(at, *streams, column, from_back, from_ahead)
    sent = call(
        pack_kernel,
        [jax.ShapeDtypeStruct((2 * PACK, 128), BF16)] * 4,
        [VMEM] * 4,
        [pltpu.VMEM((COLS, 640), BF16), pltpu.VMEM((512, 128), F32)],
        flops=2 * 1056 * 640 * 432,
        moved=5_000_000,
    )(part, rows_far, first, second)
    got = [
        sent[0],
        shift(sent[2], "x", 1),
        shift(sent[1], "x", -1),
        shift(sent[3], "x", 2),
    ]
    near = [v for block in got[:3] for v in (block, flip(block))]
    shared = (
        masks,
        gelu,
        conv_weight,
        *(v.reshape(HEADS, HEAD) for v in (conv_bias, bias_a, bias_i, decay_rate)),
        gate_a,
        gate_i,
    )
    scratch = [
        pltpu.VMEM((SIDE, LENGTH + HALO, HEAD), F32),
        pltpu.VMEM((WIDTH, LENGTH), BF16),
        pltpu.VMEM((8, 32, 128), BF16),
        pltpu.VMEM((HALO, WIDTH), F32),
        pltpu.SemaphoreType.DMA((16,)),
    ]

    def walked(heads):
        return (
            jax.ShapeDtypeStruct((heads, LENGTH, HEAD), F32),
            jax.ShapeDtypeStruct((heads, LENGTH, HEAD), F32),
            jax.ShapeDtypeStruct((2, WIDTH), F32),
        )

    states, prods, ends = call(
        near_kernel,
        walked(HEADS),
        [SMEM] + [ANY] * 6 + [VMEM] * 9,
        scratch,
        flops=2 * 128 * 2560 * 256,
        moved=20_000_000,
    )(at, *near, *shared)
    last, ends = lax.optimization_barrier((got[3], ends))
    far_states, far_prods, ends = call(
        far_kernel,
        walked(FAR),
        [SMEM] + [ANY] * 8 + [VMEM] * 10,
        scratch,
        flops=2 * 128 * 1024 * 256,
        moved=8_000_000,
    )(at, *near, last, flip(last), *shared, ends)

    two = joined(shift(ends, ctx, 1), ends)
    pairs = [shift(two, ctx, by) for by in (7, 5, 3, 1)]
    incoming = functools.reduce(joined, pairs)[1:]
    out = call(
        finish_kernel,
        jax.ShapeDtypeStruct((LENGTH, WIDTH), BF16),
        [SMEM] + [VMEM] * 5,
        moved=4_400_000,
    )(at, states, prods, far_states, far_prods, incoming)
    return out[None]


def solution(mesh):
    fine = Mesh(mesh.devices.reshape(4, 8, 4, 2), ("y", "z", "x", "c"))
    ctx, fsdp = ("y", "z"), ("x", "c")
    placed = (
        P(fsdp, ctx, None),
        P(fsdp, ctx, None),
        P(fsdp, ctx),
        P(ctx, fsdp),
        P(),
        P(),
        P(),
        P(),
        P(),
        P(),
        P(),
    )
    return jax.shard_map(
        body, mesh=fine, in_specs=placed, out_specs=P(fsdp, ctx, None), check_vma=False
    )
```

```python
import functools

import jax
import jax.numpy as jnp
from jax import lax
from jax.experimental import pallas as pl
from jax.experimental.pallas import tpu as pltpu
from jax.sharding import Mesh
from jax.sharding import PartitionSpec as P

F32 = jnp.float32
BF16 = jnp.bfloat16
VMEM = pl.BlockSpec(memory_space=pltpu.VMEM)
ANY = pl.BlockSpec(memory_space=pl.ANY)
SMEM = pl.BlockSpec(memory_space=pltpu.SMEM)

LENGTH = 128
WIDTH = 3456
DEPTH = 2560
COLS = 432
HEAD = 128
HEADS = 27
SPAN = 16
HALO = 8
PACK = COLS + 32
CUT = 208
AHEAD = 16
BLOCK = LENGTH + AHEAD
SPLIT = 64
NEAR_SIDE, FAR_SIDE = 5, 8
NEAR, FAR = 20, 8
ROWS = 4 * BLOCK


def shift(value, axis, by):
    count = lax.axis_size(axis)
    return lax.ppermute(value, axis, [(i, (i + by) % count) for i in range(count)])


def flip(value):
    return lax.ppermute(value, "c", [(0, 1), (1, 0)])


def prepare_kernel(at_ref, gate_ref, ids_ref, ahead_ref, gelu_ref, mask_ref, ids_scr):
    def head(h, carry):
        lanes = pl.ds(pl.multiple_of(h * HEAD, HEAD), HEAD)
        gelu_ref[h] = jax.nn.gelu(gate_ref[:, lanes].astype(F32), approximate=True)
        return carry

    lax.fori_loop(0, HEADS, head, 0)
    prior = ahead_ref[:, 0:LENGTH].astype(F32)[0:1]
    prior = jnp.where(at_ref[3] == 0, -1.0, prior)
    prior = jnp.broadcast_to(prior, (LENGTH, LENGTH)).T
    own = jnp.broadcast_to(ids_ref[...].astype(F32), (LENGTH, LENGTH)).T
    ids_scr[0:HALO, :] = prior[LENGTH - HALO :, :]
    ids_scr[HALO:, :] = own
    for k in range(SPAN):
        here = ids_scr[pl.ds(HALO + k, 8, stride=SPAN), :]
        for back in range(1, 4):
            there = ids_scr[pl.ds(HALO + k - back, 8, stride=SPAN), :]
            same = (here == there).astype(F32)
            mask_ref[back, 8 * k : 8 * k + 8, :] = same
            if back == 1:
                mask_ref[0, 8 * k : 8 * k + 8, :] = same


def copies(pairs, sems):
    made = [
        pltpu.make_async_copy(src, dst, sems.at[i]) for i, (src, dst) in enumerate(pairs)
    ]
    for copy in made:
        copy.start()
    return made


def across(weight, rows):
    return lax.dot_general(
        weight, rows, (((1,), (1,)), ((), ())), preferred_element_type=F32
    )


def project_kernel(at_ref, *refs):
    tokens, weights, (part_ref, far_ref) = refs[:10], refs[10:13], refs[13:]
    y = at_ref[2]

    def rows_of(half, at):
        t0, t1, t2, t3, t4 = tokens[5 * half : 5 * half + 5]
        main = [t[0:LENGTH, at] for t in (t0, t1, t2)] + [t3[:, at], t4[0:SPLIT, at]]
        rest = [t[LENGTH:BLOCK, at] for t in (t0, t1, t2)] + [t4[SPLIT:, at]]
        return jnp.concatenate(main + rest, axis=0)

    far = pl.ds(pl.multiple_of(lax.rem(y + 2, 4) * 640, 128), 640)
    for half in range(2):
        total = None
        for w_ref, back in zip(weights, (0, 3, 1)):
            at = pl.ds(pl.multiple_of(lax.rem(y + back, 4) * 640, 128), 640)
            part = across(w_ref[...], rows_of(half, at))
            total = part if total is None else total + part
        part_ref[half] = total
        far_ref[half * ROWS : (half + 1) * ROWS, :] = rows_of(half, far)


def pack_kernel(part_ref, far_ref, w0_ref, w1_ref, *refs):
    outs, (all_ref, wide_ref) = refs[:4], refs[4:]
    all_ref[0:CUT, :] = w0_ref[...]
    all_ref[CUT:COLS, :] = w1_ref[...]
    for half in range(2):
        total = part_ref[half] + across(all_ref[...], far_ref[half * ROWS : (half + 1) * ROWS, :])
        wide_ref[0:COLS, 0 : 4 * AHEAD] = total[:, 4 * LENGTH :]
        turned = [wide_ref[j * 128 : (j + 1) * 128, :].T for j in range(4)]
        top = half * PACK
        for i, out_ref in enumerate(outs):
            out_ref[top : top + COLS, :] = total[:, i * LENGTH : (i + 1) * LENGTH].astype(BF16)
            group = [t[AHEAD * (i + 1) - HALO : AHEAD * (i + 1), :] for t in turned]
            for j in range(2):
                rest = slice(top + COLS + 16 * j, top + COLS + 16 * j + 16)
                out_ref[rest, :] = jnp.concatenate(group[2 * j : 2 * j + 2], axis=0).astype(BF16)


def far_head(x):
    return jnp.minimum((lax.rem(x + 2, 4) * HEADS) // 4, HEADS - FAR)


def recur(at_ref, got, refs, far, state_ref, prod_ref, end_ref, scratch):
    (
        mask_ref,
        gelu_ref,
        taps_ref,
        bias_ref,
        bias_a_ref,
        bias_i_ref,
        rate_ref,
        gate_a_ref,
        gate_i_ref,
    ) = refs
    x_scr, main_ref, pack_ref, ahead_ref, sems = scratch
    x, c = at_ref[0], at_ref[1]
    pairs = []
    for n, ref in enumerate(got):
        place = 2 * lax.rem(x + 4 - (0, 1, 3, 2)[n // 2], 4) + (c if n % 2 == 0 else 1 - c)
        top = (n % 2) * PACK
        rows = pl.ds(pl.multiple_of(place * COLS, 16), COLS)
        pairs.append((ref.at[pl.ds(top, COLS)], main_ref.at[rows]))
        pairs.append((ref.at[pl.ds(top + COLS, 32)], pack_ref.at[place]))
    for copy in copies(pairs, sems):
        copy.wait()
    ahead = []
    for f in range(8):
        packed = pack_ref[f].astype(F32)
        ahead += [packed[8 * j : 8 * j + 8, : min(128, COLS - 128 * j)] for j in range(4)]
    ahead_ref[...] = jnp.concatenate(ahead, axis=1)

    row = lax.broadcasted_iota(jnp.int32, (8, HEAD), 0)
    start = far_head(x)

    def head(i, slot):
        h = start + i if far else lax.rem(start + FAR + i, HEADS)
        out = i if far else h
        lanes = pl.ds(pl.multiple_of(h * HEAD, HEAD), HEAD)
        at_head = pl.ds(h, 1)
        x_scr[slot, 0:HALO, :] = ahead_ref[:, lanes]
        x_scr[slot, HALO:, :] = main_ref[lanes, :].astype(F32).T
        taps = [taps_ref[n : n + 1, lanes] for n in range(4)]
        bias = bias_ref[at_head, :]
        shifted = {
            off: x_scr[slot, pl.ds(HALO + off, 8, stride=SPAN), :] for off in range(-3, SPAN)
        }
        conv = []
        for k in range(SPAN):
            total = taps[0] * shifted[k] + bias
            for back in range(1, 4):
                valid = mask_ref[back, 8 * k : 8 * k + 8, :]
                total = total + taps[back] * (shifted[k - back] * valid)
            conv.append(total)
        conv = jnp.concatenate(conv, axis=0).astype(BF16)
        gates = jnp.concatenate([gate_a_ref[h], gate_i_ref[h]], axis=1)
        both = jnp.dot(conv, gates, preferred_element_type=F32)
        rgate = jax.nn.sigmoid(both[:, :HEAD] + bias_a_ref[at_head, :])
        igate = jax.nn.sigmoid(both[:, HEAD:] + bias_i_ref[at_head, :])
        logdecay = (-8.0 * rate_ref[at_head, :]) * rgate
        decay = jnp.exp(logdecay)
        same = mask_ref[0]
        twice = 2.0 * logdecay
        series = 1.0 + twice * (
            1 / 2
            + twice
            * (1 / 6 + twice * (1 / 24 + twice * (1 / 120 + twice * (1 / 720 + twice * (1 / 5040)))))
        )
        lost = jnp.where(twice > -0.5, -twice * series, 1.0 - decay * decay)
        factor = jnp.where(same > 0.5, jnp.sqrt(lost), 1.0)
        inflow = factor * igate * conv.astype(F32)
        keep = decay * same
        prods, states = [keep[0:8]], [inflow[0:8]]
        for k in range(1, SPAN):
            part = keep[8 * k : 8 * k + 8]
            prods.append(part * prods[-1])
            states.append(part * states[-1] + inflow[8 * k : 8 * k + 8])
        prod, state = prods[-1], states[-1]
        for by in (1, 2, 4):
            before_prod = jnp.where(row >= by, pltpu.roll(prod, by, 0), 1.0)
            before_state = jnp.where(row >= by, pltpu.roll(state, by, 0), 0.0)
            state = prod * before_state + state
            prod = prod * before_prod
        end_ref[0:1, lanes] = prod[7:8]
        end_ref[1:2, lanes] = state[7:8]
        in_prod = jnp.where(row >= 1, pltpu.roll(prod, 1, 0), 1.0)
        in_state = jnp.where(row >= 1, pltpu.roll(state, 1, 0), 0.0)
        for k in range(SPAN):
            at = pl.ds(k, 8, stride=SPAN)
            gelu = gelu_ref[h, at, :]
            state_ref[out, at, :] = (states[k] + prods[k] * in_state) * gelu
            prod_ref[out, at, :] = (prods[k] * in_prod) * gelu

    side = FAR_SIDE if far else NEAR_SIDE

    def several(i, carry):
        for slot in range(side):
            head(side * i + slot, slot)
        return carry

    lax.fori_loop(0, (FAR if far else NEAR) // side, several, 0)


def near_kernel(at_ref, *refs):
    recur(at_ref, refs[:6], refs[6:15], False, *refs[15:18], refs[18:])


def far_kernel(at_ref, *refs):
    refs[20][...] = refs[17][...]
    recur(at_ref, refs[:8], refs[8:17], True, *refs[18:21], refs[21:])


def finish_kernel(at_ref, state_ref, prod_ref, far_state_ref, far_prod_ref, in_ref, out_ref):
    start = far_head(at_ref[0])

    def near(i, carry):
        for side in range(4):
            h = lax.rem(start + FAR + 4 * i + side, HEADS)
            lanes = pl.ds(pl.multiple_of(h * HEAD, HEAD), HEAD)
            out_ref[:, lanes] = (state_ref[h] + prod_ref[h] * in_ref[:, lanes]).astype(BF16)
        return carry

    def far(i, carry):
        for side in range(4):
            n = 4 * i + side
            lanes = pl.ds(pl.multiple_of((start + n) * HEAD, HEAD), HEAD)
            out_ref[:, lanes] = (far_state_ref[n] + far_prod_ref[n] * in_ref[:, lanes]).astype(
                BF16
            )
        return carry

    lax.fori_loop(0, NEAR // 4, near, 0)
    lax.fori_loop(0, FAR // 4, far, 0)


def call(kernel, outs, ins, scratch=(), room=16, flops=0, moved=0):
    return pl.pallas_call(
        kernel,
        out_shape=outs,
        in_specs=ins,
        out_specs=jax.tree.map(lambda _: VMEM, outs),
        scratch_shapes=list(scratch),
        compiler_params=pltpu.CompilerParams(vmem_limit_bytes=room * 2**20),
        cost_estimate=pl.CostEstimate(flops=flops, bytes_accessed=moved, transcendentals=0),
    )


def joined(earlier, later):
    return jnp.concatenate(
        [earlier[:1] * later[:1], later[:1] * earlier[1:] + later[1:]], axis=0
    )


def body(
    tokens,
    gate_input,
    segment_ids,
    in_weight,
    conv_weight,
    conv_bias,
    gate_a,
    gate_i,
    bias_a,
    bias_i,
    decay_rate,
):
    ctx = ("y", "z")
    own = tokens[0]
    at = jnp.stack([lax.axis_index(a) for a in ("x", "c", "y")] + [lax.axis_index(ctx)]).astype(
        jnp.int32
    )

    documents = jnp.pad(segment_ids.astype(BF16), ((0, 0), (0, DEPTH - LENGTH)))
    last = jnp.concatenate([documents, own[1 - AHEAD :]], axis=0)
    last, weight = lax.optimization_barrier((last, in_weight))
    ahead = shift(last, ctx, 1)
    copied = jnp.broadcast_to(weight[None], (8,) + weight.shape)
    column = lax.all_to_all(copied, "z", 0, 0, tiled=True).reshape(-1, COLS).T
    rows = jnp.concatenate([own, ahead], axis=0)
    one_back, one_ahead = shift(rows, "x", 1), shift(rows, "x", -1)
    gelu, masks = call(
        prepare_kernel,
        (
            jax.ShapeDtypeStruct((HEADS, LENGTH, HEAD), F32),
            jax.ShapeDtypeStruct((4, LENGTH, HEAD), F32),
        ),
        [SMEM] + [VMEM] * 3,
        [pltpu.VMEM((LENGTH + HALO, HEAD), F32)],
        room=6,
        moved=2_700_000,
    )(at, gate_input[0], segment_ids, ahead)
    column, one_back, one_ahead = lax.optimization_barrier((column, one_back, one_ahead))
    upper = shift(one_back[:SPLIT], "x", 1)
    lower = shift(one_ahead[SPLIT:], "x", -1)
    streams = [rows, one_back, one_ahead, upper, lower]
    from_back = shift(column, "y", 1)
    from_ahead = shift(column, "y", -1)
    from_back, from_ahead = lax.optimization_barrier((from_back, from_ahead))
    first = shift(from_back[:CUT], "y", 1)
    second = shift(from_ahead[CUT:], "y", -1)

    streams += [flip(t) for t in streams]
    part, rows_far = call(
        project_kernel,
        (
            jax.ShapeDtypeStruct((2, COLS, ROWS), F32),
            jax.ShapeDtypeStruct((2 * ROWS, 640), BF16),
        ),
        [SMEM] + [VMEM] * 13,
        flops=2 * 1056 * 1920 * 432,
        moved=9_000_000,
    )(at, *streams, column, from_back, from_ahead)
    sent = call(
        pack_kernel,
        [jax.ShapeDtypeStruct((2 * PACK, 128), BF16)] * 4,
        [VMEM] * 4,
        [pltpu.VMEM((COLS, 640), BF16), pltpu.VMEM((512, 128), F32)],
        flops=2 * 1056 * 640 * 432,
        moved=5_000_000,
    )(part, rows_far, first, second)
    got = [
        sent[0],
        shift(sent[2], "x", 1),
        shift(sent[1], "x", -1),
        shift(sent[3], "x", 2),
    ]
    got[1], gelu, masks = lax.optimization_barrier((got[1], gelu, masks))
    near = [v for block in got[:3] for v in (block, flip(block))]
    shared = (
        masks,
        gelu,
        conv_weight,
        *(v.reshape(HEADS, HEAD) for v in (conv_bias, bias_a, bias_i, decay_rate)),
        gate_a,
        gate_i,
    )
    scratch = [
        pltpu.VMEM((FAR_SIDE, LENGTH + HALO, HEAD), F32),
        pltpu.VMEM((WIDTH, LENGTH), BF16),
        pltpu.VMEM((8, 32, 128), BF16),
        pltpu.VMEM((HALO, WIDTH), F32),
        pltpu.SemaphoreType.DMA((16,)),
    ]

    def walked(heads):
        return (
            jax.ShapeDtypeStruct((heads, LENGTH, HEAD), F32),
            jax.ShapeDtypeStruct((heads, LENGTH, HEAD), F32),
            jax.ShapeDtypeStruct((2, WIDTH), F32),
        )

    states, prods, ends = call(
        near_kernel,
        walked(HEADS),
        [SMEM] + [ANY] * 6 + [VMEM] * 9,
        scratch,
        flops=2 * 128 * 2560 * 256,
        moved=20_000_000,
    )(at, *near, *shared)
    last, ends = lax.optimization_barrier((got[3], ends))
    far_states, far_prods, ends = call(
        far_kernel,
        walked(FAR),
        [SMEM] + [ANY] * 8 + [VMEM] * 10,
        scratch,
        flops=2 * 128 * 1024 * 256,
        moved=8_000_000,
    )(at, *near, last, flip(last), *shared, ends)

    two = joined(shift(ends, ctx, 1), ends)
    pairs = [shift(two, ctx, by) for by in (7, 5, 3, 1)]
    incoming = functools.reduce(joined, pairs)[1:]
    out = call(
        finish_kernel,
        jax.ShapeDtypeStruct((LENGTH, WIDTH), BF16),
        [SMEM] + [VMEM] * 5,
        moved=4_400_000,
    )(at, states, prods, far_states, far_prods, incoming)
    return out[None]


def solution(mesh):
    fine = Mesh(mesh.devices.reshape(4, 8, 4, 2), ("y", "z", "x", "c"))
    ctx, fsdp = ("y", "z"), ("x", "c")
    placed = (
        P(fsdp, ctx, None),
        P(fsdp, ctx, None),
        P(fsdp, ctx),
        P(ctx, fsdp),
        P(),
        P(),
        P(),
        P(),
        P(),
        P(),
        P(),
    )
    return jax.shard_map(
        body, mesh=fine, in_specs=placed, out_specs=P(fsdp, ctx, None), check_vma=False
    )
```

```python
import functools

import jax
import jax.numpy as jnp
from jax import lax
from jax.experimental import pallas as pl
from jax.experimental.pallas import tpu as pltpu
from jax.sharding import Mesh
from jax.sharding import PartitionSpec as P

F32 = jnp.float32
BF16 = jnp.bfloat16
VMEM = pl.BlockSpec(memory_space=pltpu.VMEM)
ANY = pl.BlockSpec(memory_space=pl.ANY)
SMEM = pl.BlockSpec(memory_space=pltpu.SMEM)

LENGTH = 128
WIDTH = 3456
DEPTH = 2560
COLS = 432
HEAD = 128
HEADS = 27
SPAN = 16
HALO = 8
PACK = COLS + 32
CUT = 208
AHEAD = 16
BLOCK = LENGTH + AHEAD
SPLIT = 64
SIDE = 4
NEAR, FAR = 20, 8
ROWS = 4 * BLOCK


def shift(value, axis, by):
    count = lax.axis_size(axis)
    return lax.ppermute(value, axis, [(i, (i + by) % count) for i in range(count)])


def flip(value):
    return lax.ppermute(value, "c", [(0, 1), (1, 0)])


def prepare_kernel(at_ref, gate_ref, ids_ref, ahead_ref, gelu_ref, mask_ref, ids_scr):
    def head(h, carry):
        lanes = pl.ds(pl.multiple_of(h * HEAD, HEAD), HEAD)
        gelu_ref[h] = jax.nn.gelu(gate_ref[:, lanes].astype(F32), approximate=True)
        return carry

    lax.fori_loop(0, HEADS, head, 0)
    prior = ahead_ref[:, 0:LENGTH].astype(F32)[0:1]
    prior = jnp.where(at_ref[3] == 0, -1.0, prior)
    prior = jnp.broadcast_to(prior, (LENGTH, LENGTH)).T
    own = jnp.broadcast_to(ids_ref[...].astype(F32), (LENGTH, LENGTH)).T
    ids_scr[0:HALO, :] = prior[LENGTH - HALO :, :]
    ids_scr[HALO:, :] = own
    for k in range(SPAN):
        here = ids_scr[pl.ds(HALO + k, 8, stride=SPAN), :]
        for back in range(1, 4):
            there = ids_scr[pl.ds(HALO + k - back, 8, stride=SPAN), :]
            same = (here == there).astype(F32)
            mask_ref[back, 8 * k : 8 * k + 8, :] = same
            if back == 1:
                mask_ref[0, 8 * k : 8 * k + 8, :] = same


def copies(pairs, sems):
    made = [
        pltpu.make_async_copy(src, dst, sems.at[i]) for i, (src, dst) in enumerate(pairs)
    ]
    for copy in made:
        copy.start()
    return made


def across(weight, rows):
    return lax.dot_general(
        weight, rows, (((1,), (1,)), ((), ())), preferred_element_type=F32
    )


def project_kernel(at_ref, *refs):
    tokens, weights, (part_ref, far_ref) = refs[:10], refs[10:13], refs[13:]
    y = at_ref[2]

    def rows_of(half, at):
        t0, t1, t2, t3, t4 = tokens[5 * half : 5 * half + 5]
        main = [t[0:LENGTH, at] for t in (t0, t1, t2)] + [t3[:, at], t4[0:SPLIT, at]]
        rest = [t[LENGTH:BLOCK, at] for t in (t0, t1, t2)] + [t4[SPLIT:, at]]
        return jnp.concatenate(main + rest, axis=0)

    far = pl.ds(pl.multiple_of(lax.rem(y + 2, 4) * 640, 128), 640)
    for half in range(2):
        total = None
        for w_ref, back in zip(weights, (0, 3, 1)):
            at = pl.ds(pl.multiple_of(lax.rem(y + back, 4) * 640, 128), 640)
            part = across(w_ref[...], rows_of(half, at))
            total = part if total is None else total + part
        part_ref[half] = total
        far_ref[half * ROWS : (half + 1) * ROWS, :] = rows_of(half, far)


def pack_kernel(part_ref, far_ref, w0_ref, w1_ref, *refs):
    outs, (all_ref, wide_ref) = refs[:4], refs[4:]
    all_ref[0:CUT, :] = w0_ref[...]
    all_ref[CUT:COLS, :] = w1_ref[...]
    for half in range(2):
        total = part_ref[half] + across(all_ref[...], far_ref[half * ROWS : (half + 1) * ROWS, :])
        wide_ref[0:COLS, 0 : 4 * AHEAD] = total[:, 4 * LENGTH :]
        turned = [wide_ref[j * 128 : (j + 1) * 128, :].T for j in range(4)]
        top = half * PACK
        for i, out_ref in enumerate(outs):
            out_ref[top : top + COLS, :] = total[:, i * LENGTH : (i + 1) * LENGTH].astype(BF16)
            group = [t[AHEAD * (i + 1) - HALO : AHEAD * (i + 1), :] for t in turned]
            for j in range(2):
                rest = slice(top + COLS + 16 * j, top + COLS + 16 * j + 16)
                out_ref[rest, :] = jnp.concatenate(group[2 * j : 2 * j + 2], axis=0).astype(BF16)


def far_head(x):
    return jnp.minimum((lax.rem(x + 2, 4) * HEADS) // 4, HEADS - FAR)


def recur(at_ref, got, refs, far, state_ref, prod_ref, end_ref, scratch):
    (
        mask_ref,
        gelu_ref,
        taps_ref,
        bias_ref,
        bias_a_ref,
        bias_i_ref,
        rate_ref,
        gate_a_ref,
        gate_i_ref,
    ) = refs
    x_scr, main_ref, pack_ref, ahead_ref, sems = scratch
    x, c = at_ref[0], at_ref[1]
    pairs = []
    for n, ref in enumerate(got):
        place = 2 * lax.rem(x + 4 - (0, 1, 3, 2)[n // 2], 4) + (c if n % 2 == 0 else 1 - c)
        top = (n % 2) * PACK
        rows = pl.ds(pl.multiple_of(place * COLS, 16), COLS)
        pairs.append((ref.at[pl.ds(top, COLS)], main_ref.at[rows]))
        pairs.append((ref.at[pl.ds(top + COLS, 32)], pack_ref.at[place]))
    for copy in copies(pairs, sems):
        copy.wait()
    ahead = []
    for f in range(8):
        packed = pack_ref[f].astype(F32)
        ahead += [packed[8 * j : 8 * j + 8, : min(128, COLS - 128 * j)] for j in range(4)]
    ahead_ref[...] = jnp.concatenate(ahead, axis=1)

    row = lax.broadcasted_iota(jnp.int32, (8, HEAD), 0)
    start = far_head(x)

    def head(i, slot):
        h = start + i if far else lax.rem(start + FAR + i, HEADS)
        out = i if far else h
        lanes = pl.ds(pl.multiple_of(h * HEAD, HEAD), HEAD)
        at_head = pl.ds(h, 1)
        x_scr[slot, 0:HALO, :] = ahead_ref[:, lanes]
        x_scr[slot, HALO:, :] = main_ref[lanes, :].astype(F32).T
        taps = [taps_ref[n : n + 1, lanes] for n in range(4)]
        bias = bias_ref[at_head, :]
        shifted = {
            off: x_scr[slot, pl.ds(HALO + off, 8, stride=SPAN), :] for off in range(-3, SPAN)
        }
        conv = []
        for k in range(SPAN):
            total = taps[0] * shifted[k] + bias
            for back in range(1, 4):
                valid = mask_ref[back, 8 * k : 8 * k + 8, :]
                total = total + taps[back] * (shifted[k - back] * valid)
            conv.append(total)
        conv = jnp.concatenate(conv, axis=0).astype(BF16)
        gates = jnp.concatenate([gate_a_ref[h], gate_i_ref[h]], axis=1)
        both = jnp.dot(conv, gates, preferred_element_type=F32)
        rgate = jax.nn.sigmoid(both[:, :HEAD] + bias_a_ref[at_head, :])
        igate = jax.nn.sigmoid(both[:, HEAD:] + bias_i_ref[at_head, :])
        logdecay = (-8.0 * rate_ref[at_head, :]) * rgate
        decay = jnp.exp(logdecay)
        same = mask_ref[0]
        twice = 2.0 * logdecay
        series = 1.0 + twice * (
            1 / 2
            + twice
            * (1 / 6 + twice * (1 / 24 + twice * (1 / 120 + twice * (1 / 720 + twice * (1 / 5040)))))
        )
        lost = jnp.where(twice > -0.5, -twice * series, 1.0 - decay * decay)
        factor = jnp.where(same > 0.5, jnp.sqrt(lost), 1.0)
        inflow = factor * igate * conv.astype(F32)
        keep = decay * same
        prods, states = [keep[0:8]], [inflow[0:8]]
        for k in range(1, SPAN):
            part = keep[8 * k : 8 * k + 8]
            prods.append(part * prods[-1])
            states.append(part * states[-1] + inflow[8 * k : 8 * k + 8])
        prod, state = prods[-1], states[-1]
        for by in (1, 2, 4):
            before_prod = jnp.where(row >= by, pltpu.roll(prod, by, 0), 1.0)
            before_state = jnp.where(row >= by, pltpu.roll(state, by, 0), 0.0)
            state = prod * before_state + state
            prod = prod * before_prod
        end_ref[0:1, lanes] = prod[7:8]
        end_ref[1:2, lanes] = state[7:8]
        in_prod = jnp.where(row >= 1, pltpu.roll(prod, 1, 0), 1.0)
        in_state = jnp.where(row >= 1, pltpu.roll(state, 1, 0), 0.0)
        for k in range(SPAN):
            at = pl.ds(k, 8, stride=SPAN)
            gelu = gelu_ref[h, at, :]
            state_ref[out, at, :] = (states[k] + prods[k] * in_state) * gelu
            prod_ref[out, at, :] = (prods[k] * in_prod) * gelu

    def several(i, carry):
        for slot in range(SIDE):
            head(SIDE * i + slot, slot)
        return carry

    lax.fori_loop(0, (FAR if far else NEAR) // SIDE, several, 0)


def near_kernel(at_ref, *refs):
    recur(at_ref, refs[:6], refs[6:15], False, *refs[15:18], refs[18:])


def far_kernel(at_ref, *refs):
    refs[20][...] = refs[17][...]
    recur(at_ref, refs[:8], refs[8:17], True, *refs[18:21], refs[21:])


def finish_kernel(at_ref, state_ref, prod_ref, far_state_ref, far_prod_ref, in_ref, out_ref):
    start = far_head(at_ref[0])

    def near(i, carry):
        for side in range(4):
            h = lax.rem(start + FAR + 4 * i + side, HEADS)
            lanes = pl.ds(pl.multiple_of(h * HEAD, HEAD), HEAD)
            out_ref[:, lanes] = (state_ref[h] + prod_ref[h] * in_ref[:, lanes]).astype(BF16)
        return carry

    def far(i, carry):
        for side in range(4):
            n = 4 * i + side
            lanes = pl.ds(pl.multiple_of((start + n) * HEAD, HEAD), HEAD)
            out_ref[:, lanes] = (far_state_ref[n] + far_prod_ref[n] * in_ref[:, lanes]).astype(
                BF16
            )
        return carry

    lax.fori_loop(0, NEAR // 4, near, 0)
    lax.fori_loop(0, FAR // 4, far, 0)


def call(kernel, outs, ins, scratch=(), room=16, flops=0, moved=0):
    return pl.pallas_call(
        kernel,
        out_shape=outs,
        in_specs=ins,
        out_specs=jax.tree.map(lambda _: VMEM, outs),
        scratch_shapes=list(scratch),
        compiler_params=pltpu.CompilerParams(vmem_limit_bytes=room * 2**20),
        cost_estimate=pl.CostEstimate(flops=flops, bytes_accessed=moved, transcendentals=0),
    )


def joined(earlier, later):
    return jnp.concatenate(
        [earlier[:1] * later[:1], later[:1] * earlier[1:] + later[1:]], axis=0
    )


def body(
    tokens,
    gate_input,
    segment_ids,
    in_weight,
    conv_weight,
    conv_bias,
    gate_a,
    gate_i,
    bias_a,
    bias_i,
    decay_rate,
):
    ctx = ("y", "z")
    own = tokens[0]
    at = jnp.stack([lax.axis_index(a) for a in ("x", "c", "y")] + [lax.axis_index(ctx)]).astype(
        jnp.int32
    )

    documents = jnp.pad(segment_ids.astype(BF16), ((0, 0), (0, DEPTH - LENGTH)))
    last = jnp.concatenate([documents, own[1 - AHEAD :]], axis=0)
    last, weight = lax.optimization_barrier((last, in_weight))
    ahead = shift(last, ctx, 1)
    copied = jnp.broadcast_to(weight[None], (8,) + weight.shape)
    column = lax.all_to_all(copied, "z", 0, 0, tiled=True).reshape(-1, COLS).T
    rows = jnp.concatenate([own, ahead], axis=0)
    gelu, masks = call(
        prepare_kernel,
        (
            jax.ShapeDtypeStruct((HEADS, LENGTH, HEAD), F32),
            jax.ShapeDtypeStruct((4, LENGTH, HEAD), F32),
        ),
        [SMEM] + [VMEM] * 3,
        [pltpu.VMEM((LENGTH + HALO, HEAD), F32)],
        room=6,
        moved=2_700_000,
    )(at, gate_input[0], segment_ids, ahead)
    rows, gelu, masks = lax.optimization_barrier((rows, gelu, masks))
    one_back, one_ahead = shift(rows, "x", 1), shift(rows, "x", -1)
    column, one_back, one_ahead = lax.optimization_barrier((column, one_back, one_ahead))
    upper = shift(one_back[:SPLIT], "x", 1)
    lower = shift(one_ahead[SPLIT:], "x", -1)
    streams = [rows, one_back, one_ahead, upper, lower]
    from_back = shift(column, "y", 1)
    from_ahead = shift(column, "y", -1)
    from_back, from_ahead = lax.optimization_barrier((from_back, from_ahead))
    first = shift(from_back[:CUT], "y", 1)
    second = shift(from_ahead[CUT:], "y", -1)

    streams += [flip(t) for t in streams]
    part, rows_far = call(
        project_kernel,
        (
            jax.ShapeDtypeStruct((2, COLS, ROWS), F32),
            jax.ShapeDtypeStruct((2 * ROWS, 640), BF16),
        ),
        [SMEM] + [VMEM] * 13,
        flops=2 * 1056 * 1920 * 432,
        moved=9_000_000,
    )(at, *streams, column, from_back, from_ahead)
    sent = call(
        pack_kernel,
        [jax.ShapeDtypeStruct((2 * PACK, 128), BF16)] * 4,
        [VMEM] * 4,
        [pltpu.VMEM((COLS, 640), BF16), pltpu.VMEM((512, 128), F32)],
        flops=2 * 1056 * 640 * 432,
        moved=5_000_000,
    )(part, rows_far, first, second)
    got = [
        sent[0],
        shift(sent[2], "x", 1),
        shift(sent[1], "x", -1),
        shift(sent[3], "x", 2),
    ]
    near = [v for block in got[:3] for v in (block, flip(block))]
    shared = (
        masks,
        gelu,
        conv_weight,
        *(v.reshape(HEADS, HEAD) for v in (conv_bias, bias_a, bias_i, decay_rate)),
        gate_a,
        gate_i,
    )
    scratch = [
        pltpu.VMEM((SIDE, LENGTH + HALO, HEAD), F32),
        pltpu.VMEM((WIDTH, LENGTH), BF16),
        pltpu.VMEM((8, 32, 128), BF16),
        pltpu.VMEM((HALO, WIDTH), F32),
        pltpu.SemaphoreType.DMA((16,)),
    ]

    def walked(heads):
        return (
            jax.ShapeDtypeStruct((heads, LENGTH, HEAD), F32),
            jax.ShapeDtypeStruct((heads, LENGTH, HEAD), F32),
            jax.ShapeDtypeStruct((2, WIDTH), F32),
        )

    states, prods, ends = call(
        near_kernel,
        walked(HEADS),
        [SMEM] + [ANY] * 6 + [VMEM] * 9,
        scratch,
        flops=2 * 128 * 2560 * 256,
        moved=20_000_000,
    )(at, *near, *shared)
    last, ends = lax.optimization_barrier((got[3], ends))
    far_states, far_prods, ends = call(
        far_kernel,
        walked(FAR),
        [SMEM] + [ANY] * 8 + [VMEM] * 10,
        scratch,
        flops=2 * 128 * 1024 * 256,
        moved=8_000_000,
    )(at, *near, last, flip(last), *shared, ends)

    two = joined(shift(ends, ctx, 1), ends)
    pairs = [shift(two, ctx, by) for by in (7, 5, 3, 1)]
    incoming = functools.reduce(joined, pairs)[1:]
    out = call(
        finish_kernel,
        jax.ShapeDtypeStruct((LENGTH, WIDTH), BF16),
        [SMEM] + [VMEM] * 5,
        moved=4_400_000,
    )(at, states, prods, far_states, far_prods, incoming)
    return out[None]


def solution(mesh):
    fine = Mesh(mesh.devices.reshape(4, 8, 4, 2), ("y", "z", "x", "c"))
    ctx, fsdp = ("y", "z"), ("x", "c")
    placed = (
        P(fsdp, ctx, None),
        P(fsdp, ctx, None),
        P(fsdp, ctx),
        P(ctx, fsdp),
        P(),
        P(),
        P(),
        P(),
        P(),
        P(),
        P(),
    )
    return jax.shard_map(
        body, mesh=fine, in_specs=placed, out_specs=P(fsdp, ctx, None), check_vma=False
    )
```
